128 devices in a mesh: batch: 8 (over z, core), ctx: 16 (over y, x).
Axes of the slice: x: 4, y: 4, z: 4, core: 2. Of those that a mesh axis runs over, the one named last changes fastest.
Arguments:
- tokens: bfloat16 [16384, 7168], P(('batch', 'ctx')), may hold values from -6 to 6
- q_latent: bfloat16 [16384, 1536], P(('batch', 'ctx')), may hold values from -102 to 102
- w_down_kv: bfloat16 [7168, 512], P(('batch', 'ctx')), may hold values from -0.0625 to 0.0625
- w_down_rope: bfloat16 [64, 7168], P(None, ('batch', 'ctx')), may hold values from -0.0625 to 0.0625
- kv_gain: float32 [512], replicated, may hold values from 0.1 to 1.9
- w_up_q: bfloat16 [1536, 18432], P('batch', 'ctx'), may hold values from -0.15625 to 0.15625
- w_up_kv: bfloat16 [512, 24576], P('batch', 'ctx'), may hold values from -0.25 to 0.25
- lengths: int32 [8, 4], P('batch'), may hold values from 1 to 8, 16 in all within a row
- window: int32 [8, 4], P('batch'), may hold values from 1 to 4, as said below
- flags: int32 [8, 4], P('batch'), may hold values 0 or 1
- anchor_pick: int32 [8, 4], P('batch'), may hold values from 0 to 65535
Outputs:
- attended: bfloat16 [16384, 12288], P(('batch', 'ctx'))
The draws below stay inside these ranges and needn't reach their ends.
Inputs may be any that keep to these rules, and one draw needn't show every extreme that they name: Each pack's lengths sum to 16, and some stream has exactly 8 blocks. Every pack has a stream with window 4.
All inputs are finite; a program needn't handle non-finite values. No bound on the sum of `flags` on one device may be relied on, other than what follows from the above.
Results may differ from the reference program's by a relative error of at most 0.015.
The reference program's roundings to bfloat16 on the way (of `kv_normed`, `key_rope`, `query` and `keyval`) count: a program that leaves them out, or rounds other values in their place, can miss the bound.
Values may be sent and summed in bfloat16 or wider, within the bound.
A program may use at most 128 MiB of HBM per device.

```python
import math
import jax
import jax.numpy as jnp
import numpy as np
from jax import lax

D = 7168
QL = 1536
KVL = 512
NOPE = 128
ROPE = 64
VDIM = 128
BLK = 128
WMAX = 4
STREAMS = 4
HEADS = 96
PACK = 2048
TOKENS = 16384
NB = 16
MOST = 8
N_BATCH = 8


def draw_q_latent(key, part):
    key = jax.random.fold_in(key, 11)
    first = jax.random.fold_in(key, 0)
    values = jnp.clip(jax.random.normal(first, (TOKENS, QL), jnp.float32), -4.0, 4.0)
    return values.astype(jnp.bfloat16)


def draw_window(key, part):
    key = jax.random.fold_in(key, 5)
    first, second = jax.random.split(key, 2)
    values = jax.random.randint(first, (N_BATCH, STREAMS), 1, WMAX + 1)
    widest = jax.random.randint(second, (N_BATCH, 1), 0, STREAMS)
    slots = jnp.arange(STREAMS, dtype=jnp.int32)[None, :]
    return jnp.where(slots == widest, WMAX, values).astype(jnp.int32)


def touch_ends(entries, own_key, smallest, top_value):
    spot = [jax.random.randint(jax.random.fold_in(own_key, axis), (), 0, length) for axis, length in enumerate(entries.shape)]
    main_axis = entries.shape.index(max(entries.shape))
    neighbour = spot[:main_axis] + [(spot[main_axis] + 1) % entries.shape[main_axis]] + spot[main_axis + 1:]
    return entries.at[tuple(spot)].set(smallest).at[tuple(neighbour)].set(top_value)


def level_of(stream_key, dims, shards, least, high):
    def one(position, parts):
        steps = jax.random.uniform(jax.random.fold_in(jax.random.fold_in(stream_key, 6), position), (parts,), jnp.float32, least / len(shards), high / len(shards))
        return jnp.repeat(jnp.exp(steps), dims[position] // parts).reshape((-1,) + (1,) * (len(dims) - position - 1))

    factor_of = one(*shards[0])
    for cut in shards[1:]:
        factor_of = factor_of * one(*cut)
    return factor_of


def profile(amount, total, bound, skew):
    weights = [(1 << 20) // math.isqrt(standing ** skew) + 1 for standing in range(2, amount + 1)]
    surplus, counts = total - bound - (amount - 1), [1] * (amount - 1)
    while surplus > 0:
        movable = [i for i in range(amount - 1) if counts[i] < bound]
        mass, budget = sum([weights[i] for i in movable]), surplus
        for i in movable:
            more = min(bound - counts[i], max(1, budget * weights[i] // mass), surplus)
            counts[i] = counts[i] + more
            surplus = surplus - more
    return np.array([bound] + counts)


def uneven(rng, amount, total, reach, slope):
    if amount == 2:
        one = jax.random.randint(rng, (), max(1, total - reach), min(reach, total - 1) + 1)
        return jnp.stack([one, total - one])
    tallies = jnp.asarray(profile(amount, total, reach, slope), jnp.int32)
    pairs = (amount - 1) // 2
    donor, receiver = tallies[1:1 + 2 * pairs:2], tallies[2:2 + 2 * pairs:2]
    slack = jnp.minimum(donor - 1, reach - receiver)
    passed = jax.random.randint(jax.random.fold_in(rng, 1), (pairs,), 0, 1 << 20) % (slack + 1)
    tallies = tallies.at[1:1 + 2 * pairs:2].set(donor - passed).at[2:2 + 2 * pairs:2].set(receiver + passed)
    return tallies[jax.random.permutation(jax.random.fold_in(rng, 2), amount)]


def noise(stream_key, extent, spread, reach, cuts=(), kind=jnp.bfloat16):
    loudness = level_of(stream_key, extent, cuts, -0.22, 0.18) if cuts else 1.0
    result = jax.random.normal(stream_key, extent, jnp.float32) * spread * loudness
    return jnp.minimum(jnp.maximum(result, -reach), reach).astype(kind)


def setup_inputs(seed: int = 0) -> dict:
    key_of = jax.random.split(jax.random.key(seed), 12)
    return {
        "tokens": noise(key_of[0], (TOKENS, D), 1.0, 6.0, ((0, 128),)),
        "q_latent": draw_q_latent(jax.random.fold_in(key_of[11], 71), 0),
        "w_down_kv": noise(key_of[2], (D, KVL), D ** -0.5, 0.0625, ((0, 128),)),
        "w_down_rope": noise(key_of[3], (ROPE, D), D ** -0.5, 0.0625, ((1, 128),)),
        "kv_gain": jnp.clip(1.0 + 0.18 * jax.random.normal(key_of[4], (KVL,), jnp.float32), 0.1, 1.9),
        "w_up_q": noise(key_of[5], (QL, HEADS * (NOPE + ROPE)), QL ** -0.5, 0.15625, ((0, 8), (1, 16))),
        "w_up_kv": noise(key_of[6], (KVL, HEADS * (NOPE + VDIM)), KVL ** -0.5, 0.25, ((0, 8), (1, 16))),
        "lengths": jax.vmap(lambda own: uneven(own, STREAMS, NB, MOST, 1))(jax.random.split(key_of[7], N_BATCH)).reshape((N_BATCH, STREAMS)).astype(jnp.int32),
        "window": draw_window(jax.random.fold_in(key_of[11], 71), 0),
        "flags": touch_ends((jax.random.randint(key_of[9], (N_BATCH, STREAMS), 0, 2) < 1).astype(jnp.int32), jax.random.fold_in(key_of[9], 1), 0, 1),
        "anchor_pick": touch_ends(jax.random.randint(key_of[10], (N_BATCH, STREAMS), 0, 65536), jax.random.fold_in(key_of[10], 1), 0, 65535).astype(jnp.int32),
    }


def angles(positions):
    half_dim = ROPE // 2
    freq = jnp.exp(-math.log(10000.0) * 2.0 * jnp.arange(half_dim, dtype=jnp.float32) / ROPE)
    phase = positions[:, None] * freq[None, :]
    return (jnp.cos(phase), jnp.sin(phase))

def rotate(values, cosine, sine):
    half_dim = ROPE // 2
    first = values[..., :half_dim]
    second = values[..., half_dim:]
    return jnp.concatenate([first * cosine - second * sine, first * sine + second * cosine], axis=-1)

def reference(tokens, q_latent, w_down_kv, w_down_rope, kv_gain, w_up_q, w_up_kv, lengths, window, flags, anchor_pick):
    scale = (NOPE + ROPE) ** (-0.5)
    results = []
    for pack_id in range(N_BATCH):
        inputs = tokens[pack_id * PACK:(pack_id + 1) * PACK]
        latents_q = q_latent[pack_id * PACK:(pack_id + 1) * PACK]
        stream_len = lengths[pack_id]
        ends = jnp.cumsum(stream_len).astype(jnp.int32)
        starts = (ends - stream_len).astype(jnp.int32)
        anchors = (starts + anchor_pick[pack_id] % stream_len).astype(jnp.int32)
        indices = jnp.arange(PACK, dtype=jnp.int32)
        blocks = indices // BLK
        streams = lax.optimization_barrier(jnp.sum((ends[None, :] <= blocks[:, None]).astype(jnp.int32), axis=1)).astype(jnp.int32)
        positions = (indices - starts[streams] * BLK).astype(jnp.float32)
        cosine, sine = angles(positions)
        same = streams[:, None] == streams[None, :]
        causal = indices[None, :] <= indices[:, None]
        near = blocks[:, None] - blocks[None, :] < window[pack_id][streams][:, None]
        anchored = (flags[pack_id][streams][:, None] == 1) & (blocks[None, :] == anchors[streams][:, None])
        mask = same & causal & (near | anchored)
        latent = jnp.dot(inputs, w_down_kv, preferred_element_type=jnp.float32)
        kv_normed = (latent * lax.rsqrt(lax.optimization_barrier(jnp.mean(latent * latent, axis=-1, keepdims=True)) + 1e-06) * kv_gain).astype(jnp.bfloat16)
        rope_lat = jnp.dot(inputs, w_down_rope.T, preferred_element_type=jnp.float32)
        key_rope = rotate(rope_lat, cosine, sine).astype(jnp.bfloat16)
        query = jnp.dot(latents_q, w_up_q, preferred_element_type=jnp.float32).reshape(PACK, HEADS, NOPE + ROPE)
        query = jnp.concatenate([query[..., :NOPE], rotate(query[..., NOPE:], cosine[:, None, :], sine[:, None, :])], axis=-1).astype(jnp.bfloat16)
        keyval = jnp.dot(kv_normed, w_up_kv, preferred_element_type=jnp.float32).astype(jnp.bfloat16).reshape(PACK, HEADS, NOPE + VDIM)

        def one_head(pair):
            head_query, head_keyval = pair
            scores = jnp.dot(head_query[:, :NOPE], head_keyval[:, :NOPE].T, preferred_element_type=jnp.float32)
            scores = (scores + jnp.dot(head_query[:, NOPE:], key_rope.T, preferred_element_type=jnp.float32)) * scale
            scores = jnp.where(mask, scores, -1e+30)
            maxima = lax.optimization_barrier(jnp.max(scores, axis=-1, keepdims=True))
            weights = jnp.where(mask, jnp.exp(scores - maxima), 0.0)
            totals = lax.optimization_barrier(jnp.sum(weights, axis=-1))
            mixed = jnp.dot(weights.astype(jnp.bfloat16), head_keyval[:, NOPE:], preferred_element_type=jnp.float32)
            return (mixed / totals[:, None]).astype(jnp.bfloat16)
        outputs = lax.map(one_head, (jnp.transpose(query, (1, 0, 2)), jnp.transpose(keyval, (1, 0, 2))))
        results.append(jnp.transpose(outputs, (1, 0, 2)).reshape(PACK, HEADS * VDIM))
    return jnp.concatenate(results, axis=0)
```

```python
import functools
import math

import jax
import jax.numpy as jnp
from jax import lax
from jax.experimental import pallas as pl
from jax.experimental.pallas import tpu as pltpu
from jax.sharding import PartitionSpec as P

NOPE = 128
ROPE = 64
VDIM = 128
BLK = 128
HL = 6
NB = 16
PAD = 3 * BLK
PACK = NB * BLK
MESH = pl.DeviceIdType.MESH
EXP_SCALE = (NOPE + ROPE) ** (-0.5) * math.log2(math.e)
LOW = -1e30
NT = (((1,), (1,)), ((), ()))


def shifted(c, i):
    return ((c // 4 + i // 4) % 4) * 4 + (c % 4 + i % 4) % 4


def attend_block(t, tab_ref, q_ref, kv_ref, kr_ref, write):
    start, window, anchor = tab_ref[t, 0], tab_ref[t, 1], tab_ref[t, 2]
    bias = []
    for j in range(4):
        kb = t - 3 + j
        ok = (kb >= start) & ((window > 3 - j) | (kb == anchor))
        bias.append(jnp.where(ok, 0.0, LOW))
    bias.append(jnp.where((anchor >= 0) & (anchor < t - 3), 0.0, LOW))
    first = pl.multiple_of(t * BLK, BLK)
    near_blocks, far = pl.ds(t, 4), tab_ref[t, 3]
    causal = lax.broadcasted_iota(jnp.int32, (BLK, BLK), 0) >= lax.broadcasted_iota(
        jnp.int32, (BLK, BLK), 1
    )
    for h in range(HL):
        qh = jnp.concatenate(
            [
                q_ref[pl.ds(first, BLK), h * BLK : (h + 1) * BLK],
                q_ref[pl.ds(first, BLK), (HL + h // 2) * BLK : (HL + h // 2 + 1) * BLK],
            ],
            axis=1,
        )
        part = (h % 2) * BLK
        kcol, vcol = 2 * h * BLK, (2 * h + 1) * BLK
        kn = jnp.concatenate(
            [kv_ref[near_blocks, :, kcol : kcol + BLK], kr_ref[near_blocks, :, part : part + BLK]],
            axis=2,
        ).reshape(4 * BLK, 2 * BLK)
        kf = jnp.concatenate(
            [kv_ref[far, :, kcol : kcol + BLK], kr_ref[far, :, part : part + BLK]], axis=1
        )
        near = lax.dot_general(qh, kn, NT, preferred_element_type=jnp.float32)
        tiles = [near[:, j * BLK : (j + 1) * BLK] for j in range(4)]
        tiles[3] = jnp.where(causal, tiles[3], LOW)
        tiles.append(lax.dot_general(qh, kf, NT, preferred_element_type=jnp.float32))
        top = tiles[0] + bias[0]
        for j in range(1, 5):
            top = jnp.maximum(top, tiles[j] + bias[j])
        top = jnp.max(top, axis=1, keepdims=True) * EXP_SCALE
        weights = [jnp.exp2(tiles[j] * EXP_SCALE - (top - bias[j])) for j in range(5)]
        total = weights[0]
        for j in range(1, 5):
            total = total + weights[j]
        total = jnp.sum(total, axis=1, keepdims=True)
        wn = jnp.concatenate([w.astype(jnp.bfloat16) for w in weights[:4]], axis=1)
        mixed = jnp.dot(
            wn,
            kv_ref[near_blocks, :, vcol : vcol + BLK].reshape(4 * BLK, BLK),
            preferred_element_type=jnp.float32,
        ) + jnp.dot(
            weights[4].astype(jnp.bfloat16),
            kv_ref[far, :, vcol : vcol + BLK],
            preferred_element_type=jnp.float32,
        )
        write(h, (mixed / total).astype(jnp.bfloat16))


def attention_kernel(tab_ref, q_ref, kv_ref, kr_ref, o_ref, obuf, ssem, rsem):
    c = lax.axis_index("ctx")
    barrier = pltpu.get_barrier_semaphore()
    for i in range(1, NB):
        pl.semaphore_signal(barrier, inc=1, device_id={"ctx": shifted(c, i)}, device_id_type=MESH)
    pl.semaphore_wait(barrier, NB - 1)

    own = pl.ds(pl.multiple_of(c * HL * BLK, HL * BLK), HL * BLK)

    def remote(i):
        return pltpu.make_async_remote_copy(
            src_ref=obuf.at[i],
            dst_ref=o_ref.at[:, own],
            send_sem=ssem.at[i],
            recv_sem=rsem.at[i],
            device_id={"ctx": shifted(c, i)},
            device_id_type=MESH,
        )

    def work(i):
        t = shifted(c, i)

        def write(h, value):
            obuf[i, :, h * BLK : (h + 1) * BLK] = value

        attend_block(t, tab_ref, q_ref, kv_ref, kr_ref, write)

    def step(i, carry):
        work(i)
        remote(i).start()
        return carry

    lax.fori_loop(1, NB, step, 0)
    work(0)
    local = pltpu.make_async_copy(obuf.at[0], o_ref.at[:, own], ssem.at[0])
    local.start()
    local.wait()

    def finish(i, carry):
        remote(i).wait()
        return carry

    lax.fori_loop(1, NB, finish, 0)


def attention(tab, q, kv, kr):
    return pl.pallas_call(
        attention_kernel,
        name="attention",
        out_shape=jax.ShapeDtypeStruct((BLK, NB * HL * VDIM), jnp.bfloat16),
        in_specs=[pl.BlockSpec(memory_space=pltpu.SMEM)]
        + [pl.BlockSpec(memory_space=pltpu.VMEM)] * 3,
        out_specs=pl.BlockSpec(memory_space=pl.ANY),
        scratch_shapes=[
            pltpu.VMEM((NB, BLK, HL * VDIM), jnp.bfloat16),
            pltpu.SemaphoreType.DMA((NB,)),
            pltpu.SemaphoreType.DMA((NB,)),
        ],
        compiler_params=pltpu.CompilerParams(
            collective_id=1, has_side_effects=True, vmem_limit_bytes=40 * 2**20
        ),
    )(tab, q, kv, kr)


def angles(positions):
    half_dim = ROPE // 2
    freq = jnp.exp(-math.log(10000.0) * 2.0 * jnp.arange(half_dim, dtype=jnp.float32) / ROPE)
    phase = positions[:, None] * freq[None, :]
    return (jnp.cos(phase), jnp.sin(phase))


def rotate(values, cosine, sine):
    half_dim = ROPE // 2
    first = values[..., :half_dim]
    second = values[..., half_dim:]
    return jnp.concatenate(
        [first * cosine - second * sine, first * sine + second * cosine], axis=-1
    )


def rotate_rows(values, cosine, sine):
    half_dim = ROPE // 2
    first = values[:half_dim]
    second = values[half_dim:]
    return jnp.concatenate([first * cosine - second * sine, first * sine + second * cosine], axis=0)


def block_table(stream_len, window, flags, pick):
    ends = jnp.cumsum(stream_len)
    starts = ends - stream_len
    anchors = jnp.where(flags == 1, starts + pick % stream_len, -1)
    blocks = jnp.arange(NB, dtype=jnp.int32)
    inside = (starts[None, :] <= blocks[:, None]) & (blocks[:, None] < ends[None, :])
    rows = jnp.stack([starts, window, anchors, jnp.maximum(anchors, 0) + 3], axis=1)
    return jnp.sum(jnp.where(inside[:, :, None], rows[None], 0), axis=1).astype(jnp.int32)


def per_device(
    tokens,
    q_latent,
    w_down_kv,
    w_down_rope,
    kv_gain,
    w_up_q,
    w_up_kv,
    lengths,
    window,
    flags,
    anchor_pick,
):
    ctx_index = lax.axis_index("ctx")
    table = block_table(lengths[0], window[0], flags[0], anchor_pick[0])

    latent = jnp.dot(
        tokens,
        lax.all_gather(w_down_kv, ("batch", "ctx"), axis=0, tiled=True),
        preferred_element_type=jnp.float32,
    )
    rope_part = lax.dot_general(
        lax.all_gather(w_down_rope, ("batch", "ctx"), axis=1, tiled=True),
        tokens,
        (((1,), (1,)), ((), ())),
        preferred_element_type=jnp.float32,
    )
    row_ids = jnp.arange(PACK, dtype=jnp.int32)
    row_cos, row_sin = angles(
        (row_ids - jnp.repeat(table[:, 0], BLK, total_repeat_length=PACK) * BLK).astype(jnp.float32)
    )
    cosine = lax.dynamic_slice_in_dim(row_cos, ctx_index * BLK, BLK, 0)
    sine = lax.dynamic_slice_in_dim(row_sin, ctx_index * BLK, BLK, 0)
    kv_normed = (
        latent * lax.rsqrt(jnp.mean(latent * latent, axis=-1, keepdims=True) + 1e-06) * kv_gain
    ).astype(jnp.bfloat16)
    key_rope = rotate_rows(rope_part, jnp.transpose(cosine), jnp.transpose(sine)).astype(
        jnp.bfloat16
    )
    kv_all, rope_all = (
        lax.all_gather(kv_normed, "ctx", axis=0, tiled=True),
        lax.all_gather(key_rope, "ctx", axis=1, tiled=True),
    )
    split = w_up_q.reshape(-1, HL, NOPE + ROPE)
    split = jnp.concatenate(
        [split[:, :, :NOPE].reshape(-1, HL * NOPE), split[:, :, NOPE:].reshape(-1, HL * ROPE)], axis=1
    )
    query_up, keyval_up = (
        lax.all_gather(split, "batch", axis=0, tiled=True),
        lax.all_gather(w_up_kv, "batch", axis=0, tiled=True),
    )
    pieces = lax.all_gather(q_latent, "ctx", axis=0, tiled=True)
    projected = jnp.dot(pieces, query_up, preferred_element_type=jnp.float32)
    turned = rotate(
        projected[:, HL * NOPE :].reshape(PACK, HL, ROPE), row_cos[:, None, :], row_sin[:, None, :]
    ).reshape(PACK, HL * ROPE)
    query = jnp.concatenate([projected[:, : HL * NOPE], turned], axis=1).astype(jnp.bfloat16)
    keyval = jnp.dot(kv_all, keyval_up, preferred_element_type=jnp.float32).astype(jnp.bfloat16)
    rope_rows = rope_all.T
    none = jnp.zeros_like(rope_rows)
    kr = jnp.concatenate([rope_rows, none, none, rope_rows], axis=1)
    keyval = jnp.pad(keyval, ((PAD, 0), (0, 0)))
    kr = jnp.pad(kr, ((PAD, 0), (0, 0)))
    return attention(
        table, query, keyval.reshape(NB + 3, BLK, -1), kr.reshape(NB + 3, BLK, 2 * BLK)
    )


def solution(mesh):
    return jax.shard_map(
        per_device,
        mesh=mesh,
        in_specs=(
            P(("batch", "ctx"), None),
            P(("batch", "ctx"), None),
            P(("batch", "ctx"), None),
            P(None, ("batch", "ctx")),
            P(),
            P("batch", "ctx"),
            P("batch", "ctx"),
            P("batch", None),
            P("batch", None),
            P("batch", None),
            P("batch", None),
        ),
        out_specs=P(("batch", "ctx"), None),
        check_vma=False,
    )
```

```python
import functools
import math

import jax
import jax.numpy as jnp
import numpy as np
from jax import lax
from jax.experimental import pallas as pl
from jax.experimental.pallas import tpu as pltpu
from jax.sharding import PartitionSpec as P

NOPE = 128
ROPE = 64
VDIM = 128
BLK = 128
HALF = BLK // 2
HL = 6
NB = 16
MOST = 8
KVL = 512
QL = 1536
D = 7168
SHARD = D // 128
SPAN = NB * SHARD
WQ = HL * (NOPE + ROPE)
WKV = HL * (NOPE + VDIM)
KVR = KVL + 2 * ROPE
MESH = pl.DeviceIdType.MESH
EXP_SCALE = (NOPE + ROPE) ** (-0.5) * math.log2(math.e)
LOW = -1e30
NT = (((1,), (1,)), ((), ()))
F32 = jnp.float32
BF16 = jnp.bfloat16
PARTS = ((0, 256, "xyz"), (256, 512, "yzx"), (512, 640, "zxy"))


def shifted(c, i):
    return ((c // 4 + i // 4) % 4) * 4 + (c % 4 + i % 4) % 4


class Ring:
    def __init__(self, block, half, me, plus, minus, ssem, rsem, base):
        def copy(ref, device, k):
            return pltpu.make_async_remote_copy(
                src_ref=ref,
                dst_ref=ref,
                send_sem=ssem.at[base + k],
                recv_sem=rsem.at[base + k],
                device_id=device,
                device_id_type=MESH,
            )

        self.up = copy(block(me), plus, 0)
        self.down = copy(block(me), minus, 1)
        self.on_up = copy(half((me + 3) % 4, 0), plus, 2)
        self.on_down = copy(half((me + 1) % 4, 1), minus, 3)

    def start(self):
        self.up.start()
        self.down.start()

    def middle(self):
        self.up.wait_recv()
        self.on_up.start()
        self.down.wait_recv()
        self.on_down.start()

    def end(self):
        self.on_up.wait_recv()
        self.on_down.wait_recv()

    def sent(self):
        for c in (self.up, self.down, self.on_up, self.on_down):
            c.wait_send()


def turn(v, cosine, sine):
    lane = lax.broadcasted_iota(jnp.int32, v.shape, 1)
    other = jnp.where(lane % 64 < 32, pltpu.roll(v, 96, 1), pltpu.roll(v, 32, 1))
    return v * cosine + other * sine


def attend_block(t, tab_ref, q_ref, kv_ref, kr_ref, write):
    start, window, anchor = tab_ref[t, 0], tab_ref[t, 1], tab_ref[t, 2]
    bias = []
    for j in range(4):
        kb = t - 3 + j
        ok = (kb >= start) & ((window > 3 - j) | (kb == anchor))
        bias.append(jnp.where(ok, 0.0, LOW))
    bias.append(jnp.where((anchor >= 0) & (anchor < t - 3), 0.0, LOW))
    near_blocks, far = pl.ds(t, 4), tab_ref[t, 3]
    causal = lax.broadcasted_iota(jnp.int32, (BLK, BLK), 0) >= lax.broadcasted_iota(
        jnp.int32, (BLK, BLK), 1
    )
    for h in range(HL):
        qh = jnp.concatenate(
            [
                q_ref[t, :, h * BLK : (h + 1) * BLK],
                q_ref[t, :, (HL + h // 2) * BLK : (HL + h // 2 + 1) * BLK],
            ],
            axis=1,
        )
        part = (h % 2) * BLK
        kcol, vcol = 2 * h * BLK, (2 * h + 1) * BLK
        kn = jnp.concatenate(
            [kv_ref[near_blocks, :, kcol : kcol + BLK], kr_ref[near_blocks, :, part : part + BLK]],
            axis=2,
        ).reshape(4 * BLK, 2 * BLK)
        kf = jnp.concatenate(
            [kv_ref[far, :, kcol : kcol + BLK], kr_ref[far, :, part : part + BLK]], axis=1
        )
        near = lax.dot_general(qh, kn, NT, preferred_element_type=F32)
        tiles = [near[:, j * BLK : (j + 1) * BLK] for j in range(4)]
        tiles[3] = jnp.where(causal, tiles[3], LOW)
        tiles.append(lax.dot_general(qh, kf, NT, preferred_element_type=F32))
        top = tiles[0] + bias[0]
        for j in range(1, 5):
            top = jnp.maximum(top, tiles[j] + bias[j])
        top = jnp.max(top, axis=1, keepdims=True) * EXP_SCALE
        weights = [jnp.exp2(tiles[j] * EXP_SCALE - (top - bias[j])) for j in range(5)]
        total = weights[0]
        for j in range(1, 5):
            total = total + weights[j]
        total = jnp.sum(total, axis=1, keepdims=True)
        wn = jnp.concatenate([w.astype(BF16) for w in weights[:4]], axis=1)
        mixed = jnp.dot(
            wn,
            kv_ref[near_blocks, :, vcol : vcol + BLK].reshape(4 * BLK, BLK),
            preferred_element_type=F32,
        ) + jnp.dot(
            weights[4].astype(BF16),
            kv_ref[far, :, vcol : vcol + BLK],
            preferred_element_type=F32,
        )
        write(h, (mixed / total).astype(BF16))


def spread(tok_ref, col, store):
    lane = lax.broadcasted_iota(jnp.int32, (BLK, BLK), 1)
    for p in range(8):
        tile, off = divmod(2 * SHARD * p, BLK)
        v = tok_ref[:, pl.ds(col + tile * BLK, BLK)].astype(F32)
        if off:
            v = pltpu.roll(v, BLK - off, 1)
            if tile < 6:
                after = tok_ref[:, pl.ds(col + (tile + 1) * BLK, BLK)].astype(F32)
                v = jnp.where(lane < BLK - off, v, pltpu.roll(after, BLK - off, 1))
        store(p, jnp.where(lane < 64, v, pltpu.roll(v, 8, 1)).astype(BF16))


def kernel(
    tab_ref,
    tok_ref,
    ql_ref,
    wd_ref,
    wq_ref,
    wkv_ref,
    gain_ref,
    cos_ref,
    sin_ref,
    o_ref,
    wd_a,
    wd_b,
    wd_c,
    ql_a,
    ql_b,
    kvn_a,
    kvn_b,
    wq,
    wkv,
    tok,
    tok_out,
    part,
    part_in,
    q,
    kv,
    kr,
    obuf,
    ssem,
    rsem,
    csem,
    cother,
    asem,
    arem,
):
    b, c = lax.axis_index("batch"), lax.axis_index("ctx")
    z, core, y, x = b // 2, b % 2, c // 4, c % 4
    at = {"x": x, "y": y, "z": z}

    def neighbour(axis, by):
        if axis == "x":
            return {"ctx": y * 4 + (x + by) % 4}
        if axis == "y":
            return {"ctx": ((y + by) % 4) * 4 + x}
        return {"batch": ((z + by) % 4) * 2 + core}

    partner = {"batch": z * 2 + 1 - core}

    barrier = pltpu.get_barrier_semaphore()
    peers = [{"ctx": shifted(c, i)} for i in range(1, NB)]
    peers += [neighbour("z", 1), neighbour("z", 3), partner]
    for peer in peers:
        pl.semaphore_signal(barrier, inc=1, device_id=peer, device_id_type=MESH)

    used = [0]

    def ring(axis, block, half):
        base = used[0]
        used[0] += 4
        return Ring(
            block, half, at[axis], neighbour(axis, 1), neighbour(axis, 3), ssem, rsem, base
        )

    def gather(buf, order, mid, dims="yx"):
        stages = []
        for i, axis in enumerate(order):
            done = order[:i]

            def block(k, axis=axis, done=done):
                index = [k if a == axis else slice(None) if a in done else at[a] for a in dims]
                return buf.at[tuple(index)]

            def half(k, h, axis=axis, done=done):
                index = [k if a == axis else slice(None) if a in done else at[a] for a in dims]
                return buf.at[tuple(index) + (pl.ds(h * mid, mid),)]

            stages.append(ring(axis, block, half))
        return stages

    def swap(src, dst, k):
        return pltpu.make_async_remote_copy(
            src_ref=src,
            dst_ref=dst,
            send_sem=csem.at[k],
            recv_sem=cother.at[k],
            device_id=partner,
            device_id_type=MESH,
        )

    wd_buf = (wd_a, wd_b, wd_c)
    wd = [gather(buf, order, 32, "zyx") for buf, (_, _, order) in zip(wd_buf, PARTS)]
    ql = [gather(ql_a, "xy", 32), gather(ql_b, "yx", 32)]
    kvn = [gather(kvn_a, "xy", 32), gather(kvn_b, "yx", 32)]

    def up_ring(buf, rows):
        return ring(
            "z",
            lambda k: buf.at[k, core],
            lambda k, h: buf.at[k, core, pl.ds(h * rows // 2, rows // 2)],
        )

    wq_ring, wkv_ring = up_ring(wq, QL // 8), up_ring(wkv, KVL // 8)

    for buf, (lo, hi, _) in zip(wd_buf, PARTS):
        buf[z, y, x] = wd_ref[:, lo:hi]
    ql_a[y, x] = ql_ref[:HALF]
    ql_b[y, x] = ql_ref[HALF:]
    wkv[z, core] = wkv_ref[...]
    wq[z, core] = wq_ref[...]

    pl.semaphore_wait(barrier, len(peers))
    for g in wd:
        g[0].start()
    for g in ql:
        g[0].start()
    wkv_ring.start()

    def spread_out(i, carry):
        def keep(p, v):
            tok[i, 0, :, p * BLK : (p + 1) * BLK] = v

        def give(p, v):
            tok_out[i, :, p * BLK : (p + 1) * BLK] = v

        spread(tok_ref, pl.multiple_of((i * 2 + core) * SPAN, BLK), keep)
        spread(tok_ref, pl.multiple_of((i * 2 + 1 - core) * SPAN, BLK), give)
        return carry

    for g in wd:
        g[0].middle()
    lax.fori_loop(0, 4, spread_out, 0)
    tok_swap = swap(tok_out, tok.at[:, 1], 0)
    tok_swap.start()
    for g in wd:
        g[0].end()
        g[1].start()
    for g in ql:
        g[0].middle()
    for g in wd:
        g[1].middle()
    for g in wd:
        g[1].end()
        g[2].start()
    for g in ql:
        g[0].end()
        g[1].start()
    wkv_ring.middle()
    wq_ring.start()

    kv[0:3] = jnp.zeros((3, BLK, WKV), BF16)
    kr[0:3] = jnp.zeros((3, BLK, 2 * BLK), BF16)

    for g in wd:
        g[2].middle()
    wkv_ring.end()
    wkv_swap = [swap(wkv.at[i, core], wkv.at[i, core], 1 + i) for i in range(4)]
    for s in wkv_swap:
        s.start()
    tok_swap.wait_recv()
    for g in wd:
        g[2].end()

    def down(i, carry):
        t = tok[i].reshape(2 * BLK, 8 * BLK)
        for buf, (lo, hi, _) in zip(wd_buf, PARTS):
            w = buf[i].reshape(NB * 64, hi - lo)
            part[:, :, lo:hi] += jnp.dot(t, w, preferred_element_type=F32).reshape(2, BLK, hi - lo)
        return carry

    part[...] = jnp.zeros_like(part)
    lax.fori_loop(0, 4, down, 0)
    part_swap = swap(part.at[1], part_in, 5)
    part_swap.start()
    for g in ql:
        g[1].middle()
    wq_ring.middle()
    part_swap.wait_recv()
    both = part[0] + part_in[...]
    latent = both[:, :KVL]
    norm = lax.rsqrt(jnp.mean(latent * latent, axis=1, keepdims=True) + 1e-06)
    place = tab_ref[c, 4]
    own = jnp.concatenate(
        [latent * norm * gain_ref[...], turn(both[:, KVL:], cos_ref[place], sin_ref[place])], axis=1
    ).astype(BF16)
    kvn_a[y, x] = own[:HALF]
    kvn_b[y, x] = own[HALF:]
    for g in kvn:
        g[0].start()
    wq_ring.end()
    wq_swap = [swap(wq.at[i, core], wq.at[i, core], 6 + i) for i in range(4)]
    for s in wq_swap:
        s.start()
    for g in kvn:
        g[0].middle()
    for g in kvn:
        g[0].end()
        g[1].start()
    for g in ql:
        g[1].end()
    for g in kvn:
        g[1].middle()
    for s in wq_swap:
        s.wait_recv()

    def queries(buf, row):
        rows = slice(row, row + HALF)

        def body(i, carry):
            left = buf[i].reshape(4 * HALF, QL)
            weight = wq[...].reshape(QL, WQ)
            plain = jnp.dot(left, weight[:, : HL * NOPE], preferred_element_type=F32)
            q[pl.ds(4 * i, 4), rows, : HL * NOPE] = plain.astype(BF16).reshape(4, HALF, HL * NOPE)
            rope = jnp.dot(left, weight[:, HL * NOPE :], preferred_element_type=F32)
            for k in range(4):
                t = 4 * i + k
                place = tab_ref[t, 4]
                cosine, sine = cos_ref[place, rows], sin_ref[place, rows]
                for j in range(HL // 2):
                    v = rope[k * HALF : (k + 1) * HALF, j * BLK : (j + 1) * BLK]
                    lo = (HL + j) * BLK
                    q[t, rows, lo : lo + BLK] = turn(v, cosine, sine).astype(BF16)
            return carry

        lax.fori_loop(0, 4, body, 0)

    queries(ql_a, 0)
    queries(ql_b, HALF)
    for g in kvn:
        g[1].end()
    for s in wkv_swap:
        s.wait_recv()

    lane = lax.broadcasted_iota(jnp.int32, (4, HALF, BLK), 2)

    def keyvals(buf, row):
        rows = slice(row, row + HALF)

        def body(i, carry):
            left = buf[i]
            weight = wkv[...].reshape(KVL, WKV)
            blocks = pl.ds(3 + 4 * i, 4)
            value = jnp.dot(
                left[:, :, :KVL].reshape(4 * HALF, KVL), weight, preferred_element_type=F32
            )
            kv[blocks, rows, :] = value.astype(BF16).reshape(4, HALF, WKV)
            turned = left[:, :, KVL:].astype(F32)
            kr[blocks, rows, :BLK] = jnp.where(lane < ROPE, turned, 0.0).astype(BF16)
            kr[blocks, rows, BLK:] = jnp.where(lane < ROPE, 0.0, turned).astype(BF16)
            return carry

        lax.fori_loop(0, 4, body, 0)

    keyvals(kvn_a, 0)
    keyvals(kvn_b, HALF)

    columns = pl.ds(pl.multiple_of(c * HL * BLK, HL * BLK), HL * BLK)

    def remote(i):
        return pltpu.make_async_remote_copy(
            src_ref=obuf.at[i],
            dst_ref=o_ref.at[:, columns],
            send_sem=asem.at[i],
            recv_sem=arem.at[i],
            device_id={"ctx": shifted(c, i)},
            device_id_type=MESH,
        )

    def work(i):
        def write(h, value):
            obuf[i, :, h * BLK : (h + 1) * BLK] = value

        attend_block(shifted(c, i), tab_ref, q, kv, kr, write)

    def step(i, carry):
        work(i)
        remote(i).start()
        return carry

    lax.fori_loop(1, NB, step, 0)
    work(0)
    local = pltpu.make_async_copy(obuf.at[0], o_ref.at[:, columns], asem.at[0])
    local.start()
    for g in wd + ql + kvn + [[wq_ring, wkv_ring]]:
        for s in g:
            s.sent()
    for s in [tok_swap, part_swap] + wkv_swap + wq_swap:
        s.wait_send()
    local.wait()

    def finish(i, carry):
        remote(i).wait()
        return carry

    lax.fori_loop(1, NB, finish, 0)


def tables():
    freq = np.exp(-math.log(10000.0) * 2.0 * np.arange(32, dtype=np.float32) / ROPE).astype(np.float32)
    phase = np.arange(MOST * BLK, dtype=np.float32)[:, None] * freq[None, :]
    cosine, sine = np.cos(phase.astype(np.float64)), np.sin(phase.astype(np.float64))
    shape = (MOST, BLK, BLK)
    return (
        np.concatenate([cosine] * 4, axis=1).astype(np.float32).reshape(shape),
        np.concatenate([-sine, sine, -sine, sine], axis=1).astype(np.float32).reshape(shape),
    )


def block_table(stream_len, window, flags, pick):
    slots = jnp.arange(4, dtype=jnp.int32)
    starts = jnp.sum(jnp.where(slots[None, :] < slots[:, None], stream_len[None, :], 0), axis=1)
    anchors = jnp.where(flags == 1, starts + pick % stream_len, -1)
    blocks = jnp.arange(NB, dtype=jnp.int32)
    inside = (starts[None, :] <= blocks[:, None]) & (
        blocks[:, None] < (starts + stream_len)[None, :]
    )
    rows = jnp.stack([starts, window, anchors, jnp.maximum(anchors, 0) + 3], axis=1)
    rows = jnp.concatenate(
        [jnp.broadcast_to(rows[None], (NB, 4, 4)), (blocks[:, None] - starts[None, :])[:, :, None]],
        axis=2,
    )
    return jnp.sum(jnp.where(inside[:, :, None], rows, 0), axis=1).astype(jnp.int32)


def per_device(
    tokens,
    q_latent,
    w_down_kv,
    w_down_rope,
    kv_gain,
    w_up_q,
    w_up_kv,
    lengths,
    window,
    flags,
    anchor_pick,
):
    table = block_table(lengths[0], window[0], flags[0], anchor_pick[0])
    rope = w_down_rope.T
    wd = jnp.pad(jnp.concatenate([w_down_kv, rope, rope], axis=1), ((0, 64 - SHARD), (0, 0)))
    split = w_up_q.reshape(-1, HL, NOPE + ROPE)
    wq = jnp.concatenate(
        [split[:, :, :NOPE].reshape(-1, HL * NOPE), split[:, :, NOPE:].reshape(-1, HL * ROPE)], axis=1
    )
    cosine, sine = tables()
    vmem = pl.BlockSpec(memory_space=pltpu.VMEM)
    n_sem = 4 * 19
    return pl.pallas_call(
        kernel,
        name="mla",
        out_shape=jax.ShapeDtypeStruct((BLK, NB * HL * VDIM), BF16),
        in_specs=[pl.BlockSpec(memory_space=pltpu.SMEM)] + [vmem] * 8,
        out_specs=pl.BlockSpec(memory_space=pl.ANY),
        scratch_shapes=[
            pltpu.VMEM((4, 4, 4, 64, 256), BF16),
            pltpu.VMEM((4, 4, 4, 64, 256), BF16),
            pltpu.VMEM((4, 4, 4, 64, 128), BF16),
            pltpu.VMEM((4, 4, HALF, QL), BF16),
            pltpu.VMEM((4, 4, HALF, QL), BF16),
            pltpu.VMEM((4, 4, HALF, KVR), BF16),
            pltpu.VMEM((4, 4, HALF, KVR), BF16),
            pltpu.VMEM((4, 2, QL // 8, WQ), BF16),
            pltpu.VMEM((4, 2, KVL // 8, WKV), BF16),
            pltpu.VMEM((4, 2, BLK, 8 * BLK), BF16),
            pltpu.VMEM((4, BLK, 8 * BLK), BF16),
            pltpu.VMEM((2, BLK, KVR), F32),
            pltpu.VMEM((BLK, KVR), F32),
            pltpu.VMEM((NB, BLK, WQ), BF16),
            pltpu.VMEM((NB + 3, BLK, WKV), BF16),
            pltpu.VMEM((NB + 3, BLK, 2 * BLK), BF16),
            pltpu.VMEM((NB, BLK, HL * VDIM), BF16),
            pltpu.SemaphoreType.DMA((n_sem,)),
            pltpu.SemaphoreType.DMA((n_sem,)),
            pltpu.SemaphoreType.DMA((10,)),
            pltpu.SemaphoreType.DMA((10,)),
            pltpu.SemaphoreType.DMA((NB,)),
            pltpu.SemaphoreType.DMA((NB,)),
        ],
        compiler_params=pltpu.CompilerParams(
            collective_id=1, has_side_effects=True, vmem_limit_bytes=56 * 2**20
        ),
    )(table, tokens, q_latent, wd, wq, w_up_kv, kv_gain.reshape(1, KVL), cosine, sine)


def solution(mesh):
    return jax.shard_map(
        per_device,
        mesh=mesh,
        in_specs=(
            P(("batch", "ctx"), None),
            P(("batch", "ctx"), None),
            P(("batch", "ctx"), None),
            P(None, ("batch", "ctx")),
            P(),
            P("batch", "ctx"),
            P("batch", "ctx"),
            P("batch", None),
            P("batch", None),
            P("batch", None),
            P("batch", None),
        ),
        out_specs=P(("batch", "ctx"), None),
        check_vma=False,
    )
```

```python
import functools
import math

import jax
import jax.numpy as jnp
import numpy as np
from jax import lax
from jax.experimental import pallas as pl
from jax.experimental.pallas import tpu as pltpu
from jax.sharding import PartitionSpec as P

NOPE = 128
ROPE = 64
VDIM = 128
BLK = 128
HALF = BLK // 2
HL = 6
NB = 16
MOST = 8
KVL = 512
QL = 1536
D = 7168
SHARD = D // 128
SPAN = NB * SHARD
WQ = HL * (NOPE + ROPE)
WKV = HL * (NOPE + VDIM)
KVR = KVL + 2 * ROPE
MESH = pl.DeviceIdType.MESH
EXP_SCALE = (NOPE + ROPE) ** (-0.5) * math.log2(math.e)
LOW = -1e30
NT = (((1,), (1,)), ((), ()))
F32 = jnp.float32
BF16 = jnp.bfloat16
ORDERS = ("xyz", "yzx", "zxy")
PIECE = 96


def shifted(c, i):
    return ((c // 4 + i // 4) % 4) * 4 + (c % 4 + i % 4) % 4


class Ring:
    def __init__(self, block, half, me, plus, minus, ssem, rsem, base):
        def copy(ref, device, k):
            return pltpu.make_async_remote_copy(
                src_ref=ref,
                dst_ref=ref,
                send_sem=ssem.at[base + k],
                recv_sem=rsem.at[base + k],
                device_id=device,
                device_id_type=MESH,
            )

        self.up = copy(block(me), plus, 0)
        self.down = copy(block(me), minus, 1)
        self.on_up = copy(half((me + 3) % 4, 0), plus, 2)
        self.on_down = copy(half((me + 1) % 4, 1), minus, 3)

    def start(self):
        self.up.start()
        self.down.start()

    def middle(self):
        self.up.wait_recv()
        self.on_up.start()
        self.down.wait_recv()
        self.on_down.start()

    def end(self):
        self.on_up.wait_recv()
        self.on_down.wait_recv()

    def sent(self):
        for c in (self.up, self.down, self.on_up, self.on_down):
            c.wait_send()


class Direct:
    def __init__(self, block, me, others, ssem, rsem, base):
        ref = block(me)
        self.copies = [
            pltpu.make_async_remote_copy(
                src_ref=ref,
                dst_ref=ref,
                send_sem=ssem.at[base + k],
                recv_sem=rsem.at[base + k],
                device_id=other,
                device_id_type=MESH,
            )
            for k, other in enumerate(others)
        ]

    def start(self):
        for c in self.copies:
            c.start()

    def middle(self):
        pass

    def end(self):
        for c in self.copies:
            c.wait_recv()

    def sent(self):
        for c in self.copies:
            c.wait_send()


def block_table(len_ref, window_ref, flag_ref, pick_ref, tab_ref):
    starts, anchors, start = [], [], 0
    for s in range(4):
        length, rest = len_ref[0, s], pick_ref[0, s]
        for k in range(16, -1, -1):
            rest = jnp.where(rest >= length * 2**k, rest - length * 2**k, rest)
        anchors.append(jnp.where(flag_ref[0, s] == 1, start + rest, -1))
        starts.append(start)
        start = start + length
    for t in range(NB):
        row = [0, window_ref[0, 0], anchors[0]]
        for s in range(1, 4):
            later = starts[s] <= t
            row = [
                jnp.where(later, new, old)
                for new, old in zip((starts[s], window_ref[0, s], anchors[s]), row)
            ]
        for k in range(3):
            tab_ref[t, k] = row[k]
        tab_ref[t, 3] = jnp.clip(row[2], 0, NB - 1) + 3
        tab_ref[t, 4] = jnp.clip(t - row[0], 0, MOST - 1)


def turn(v, cosine, sine):
    lane = lax.broadcasted_iota(jnp.int32, v.shape, 1)
    other = jnp.where(lane % 64 < 32, pltpu.roll(v, 96, 1), pltpu.roll(v, 32, 1))
    return v * cosine + other * sine


def attend_block(t, tab_ref, q_ref, kv_ref, kr_ref, write):
    start, window, anchor = tab_ref[t, 0], tab_ref[t, 1], tab_ref[t, 2]
    bias = []
    for j in range(4):
        kb = t - 3 + j
        ok = (kb >= start) & ((window > 3 - j) | (kb == anchor))
        bias.append(jnp.where(ok, 0.0, LOW))
    bias.append(jnp.where((anchor >= 0) & (anchor < t - 3), 0.0, LOW))
    near_blocks, far = pl.ds(t, 4), tab_ref[t, 3]
    causal = lax.broadcasted_iota(jnp.int32, (BLK, BLK), 0) >= lax.broadcasted_iota(
        jnp.int32, (BLK, BLK), 1
    )
    for h in range(HL):
        qh = jnp.concatenate(
            [
                q_ref[t, :, h * BLK : (h + 1) * BLK],
                q_ref[t, :, (HL + h // 2) * BLK : (HL + h // 2 + 1) * BLK],
            ],
            axis=1,
        )
        part = (h % 2) * BLK
        kcol, vcol = 2 * h * BLK, (2 * h + 1) * BLK
        kn = jnp.concatenate(
            [kv_ref[near_blocks, :, kcol : kcol + BLK], kr_ref[near_blocks, :, part : part + BLK]],
            axis=2,
        ).reshape(4 * BLK, 2 * BLK)
        kf = jnp.concatenate(
            [kv_ref[far, :, kcol : kcol + BLK], kr_ref[far, :, part : part + BLK]], axis=1
        )
        near = lax.dot_general(qh, kn, NT, preferred_element_type=F32)
        tiles = [near[:, j * BLK : (j + 1) * BLK] for j in range(4)]
        tiles[3] = jnp.where(causal, tiles[3], LOW)
        tiles.append(lax.dot_general(qh, kf, NT, preferred_element_type=F32))
        top = tiles[0] + bias[0]
        for j in range(1, 5):
            top = jnp.maximum(top, tiles[j] + bias[j])
        top = jnp.max(top, axis=1, keepdims=True) * EXP_SCALE
        weights = [jnp.exp2(tiles[j] * EXP_SCALE - (top - bias[j])) for j in range(5)]
        total = weights[0]
        for j in range(1, 5):
            total = total + weights[j]
        total = jnp.sum(total, axis=1, keepdims=True)
        wn = jnp.concatenate([w.astype(BF16) for w in weights[:4]], axis=1)
        mixed = jnp.dot(
            wn,
            kv_ref[near_blocks, :, vcol : vcol + BLK].reshape(4 * BLK, BLK),
            preferred_element_type=F32,
        ) + jnp.dot(
            weights[4].astype(BF16),
            kv_ref[far, :, vcol : vcol + BLK],
            preferred_element_type=F32,
        )
        write(h, (mixed / total).astype(BF16))


def spread(tok_ref, col, store):
    lane = lax.broadcasted_iota(jnp.int32, (BLK, BLK), 1)
    for p in range(8):
        tile, off = divmod(2 * SHARD * p, BLK)
        v = tok_ref[:, pl.ds(col + tile * BLK, BLK)].astype(F32)
        if off:
            v = pltpu.roll(v, BLK - off, 1)
            if tile < 6:
                after = tok_ref[:, pl.ds(col + (tile + 1) * BLK, BLK)].astype(F32)
                v = jnp.where(lane < BLK - off, v, pltpu.roll(after, BLK - off, 1))
        store(p, jnp.where(lane < 64, v, pltpu.roll(v, 8, 1)).astype(BF16))


def kernel(
    len_ref,
    window_ref,
    flag_ref,
    pick_ref,
    tok_ref,
    ql_ref,
    wd_ref,
    wr_ref,
    wq_ref,
    wkv_ref,
    gain_ref,
    cos_ref,
    sin_ref,
    o_ref,
    wd_a,
    wd_b,
    wd_c,
    ql_a,
    ql_b,
    kvn_a,
    kvn_b,
    wq,
    wkv,
    tok,
    tok_out,
    part,
    part_in,
    q,
    kv,
    kr,
    obuf,
    tab_ref,
    ssem,
    rsem,
    csem,
    cother,
    asem,
    arem,
):
    b, c = lax.axis_index("batch"), lax.axis_index("ctx")
    z, core, y, x = b // 2, b % 2, c // 4, c % 4
    at = {"x": x, "y": y, "z": z}

    def neighbour(axis, by):
        if axis == "x":
            return {"ctx": y * 4 + (x + by) % 4}
        if axis == "y":
            return {"ctx": ((y + by) % 4) * 4 + x}
        return {"batch": ((z + by) % 4) * 2 + core}

    partner = {"batch": z * 2 + 1 - core}

    barrier = pltpu.get_barrier_semaphore()
    peers = [{"ctx": shifted(c, i)} for i in range(1, NB)]
    peers += [neighbour("z", 1), neighbour("z", 2), neighbour("z", 3), partner]
    for peer in peers:
        pl.semaphore_signal(barrier, inc=1, device_id=peer, device_id_type=MESH)

    used = [0]

    def ring(axis, block, half):
        base = used[0]
        used[0] += 4
        return Ring(
            block, half, at[axis], neighbour(axis, 1), neighbour(axis, 3), ssem, rsem, base
        )

    def direct(axis, block):
        base = used[0]
        used[0] += 4
        return Direct(block, at[axis], [neighbour(axis, k) for k in (1, 2, 3)], ssem, rsem, base)

    def gather(buf, order, mid, dims="yx", quick=0):
        stages = []
        for i, axis in enumerate(order):
            done = order[:i]

            def block(k, axis=axis, done=done):
                index = [k if a == axis else slice(None) if a in done else at[a] for a in dims]
                return buf.at[tuple(index)]

            def half(k, h, axis=axis, done=done):
                index = [k if a == axis else slice(None) if a in done else at[a] for a in dims]
                return buf.at[tuple(index) + (pl.ds(h * mid, mid),)]

            stages.append(direct(axis, block) if i < quick else ring(axis, block, half))
        return stages

    def swap(src, dst, k):
        return pltpu.make_async_remote_copy(
            src_ref=src,
            dst_ref=dst,
            send_sem=csem.at[k],
            recv_sem=cother.at[k],
            device_id=partner,
            device_id_type=MESH,
        )

    wd_buf = (wd_a, wd_b, wd_c)
    wd = [gather(buf, order, PIECE // 2, "zyx", 2) for buf, order in zip(wd_buf, ORDERS)]
    ql = [gather(ql_a, "xy", 32), gather(ql_b, "yx", 32)]
    kvn = [gather(kvn_a, "xy", 32, quick=1), gather(kvn_b, "yx", 32, quick=1)]

    def up_ring(buf, rows):
        return ring(
            "z",
            lambda k: buf.at[k, core],
            lambda k, h: buf.at[k, core, pl.ds(h * rows // 2, rows // 2)],
        )

    wq_ring, wkv_ring = up_ring(wq, QL // 8), up_ring(wkv, KVL // 8)

    down_rows = jnp.concatenate([wd_ref[...].astype(F32), jnp.zeros((64 - SHARD, KVL), F32)], axis=0)
    rope_rows = lax.dot_general(
        (
            lax.broadcasted_iota(jnp.int32, (64, SHARD), 0)
            == lax.broadcasted_iota(jnp.int32, (64, SHARD), 1)
        ).astype(F32).astype(BF16),
        jnp.concatenate([wr_ref[...], wr_ref[...]], axis=0),
        NT,
        preferred_element_type=F32,
    )
    lane = lax.broadcasted_iota(jnp.int32, (32, BLK), 1)
    pieces = (
        (down_rows[:, :128], down_rows[:32, 128:256]),
        (down_rows[:, 256:384], down_rows[32:, 128:256]),
        (down_rows[:, 384:], jnp.where(lane < 64, rope_rows[:32], rope_rows[32:])),
    )
    for buf, piece in zip(wd_buf, pieces):
        buf[z, y, x] = jnp.concatenate(piece, axis=0).astype(BF16)
    ql_a[y, x] = ql_ref[:HALF]
    ql_b[y, x] = ql_ref[HALF:]
    wkv[z, core] = wkv_ref[...]
    wq[z, core] = wq_ref[...]

    block_table(len_ref, window_ref, flag_ref, pick_ref, tab_ref)
    pl.semaphore_wait(barrier, len(peers))
    for g in wd:
        g[0].start()
    for g in ql:
        g[0].start()
    wkv_ring.start()

    def spread_out(i, carry):
        def keep(p, v):
            tok[i, 0, :, p * BLK : (p + 1) * BLK] = v

        def give(p, v):
            tok_out[i, :, p * BLK : (p + 1) * BLK] = v

        spread(tok_ref, pl.multiple_of((i * 2 + core) * SPAN, BLK), keep)
        spread(tok_ref, pl.multiple_of((i * 2 + 1 - core) * SPAN, BLK), give)
        return carry

    for g in wd:
        g[0].middle()
    lax.fori_loop(0, 4, spread_out, 0)
    tok_swap = swap(tok_out, tok.at[:, 1], 0)
    tok_swap.start()
    for g in wd:
        g[0].end()
        g[1].start()
    for g in ql:
        g[0].middle()
    for g in wd:
        g[1].middle()
    for g in wd:
        g[1].end()
        g[2].start()
    for g in ql:
        g[0].end()
        g[1].start()
    wkv_ring.middle()
    wq_ring.start()

    kv[0:3] = jnp.zeros((3, BLK, WKV), BF16)
    kr[0:3] = jnp.zeros((3, BLK, 2 * BLK), BF16)

    for g in wd:
        g[2].middle()
    wkv_ring.end()
    wkv_swap = [swap(wkv.at[i, core], wkv.at[i, core], 1 + i) for i in range(4)]
    for s in wkv_swap:
        s.start()
    tok_swap.wait_recv()
    for g in wd:
        g[2].end()

    def down(i, carry):
        t = tok[i].reshape(2 * BLK, 8 * BLK)
        first, second, third = (buf[i].reshape(NB, PIECE, BLK) for buf in wd_buf)
        shared = jnp.concatenate([first[:, 64:], second[:, 64:]], axis=1)
        packed = third[:, 64:].astype(F32)
        moved = pltpu.roll(packed.reshape(NB * 32, BLK), 64, 1).reshape(NB, 32, BLK)
        rope = jnp.concatenate([packed, moved], axis=1).astype(BF16)
        for lo, w in (
            (0, jnp.concatenate([first[:, :64], shared], axis=2)),
            (256, jnp.concatenate([second[:, :64], third[:, :64]], axis=2)),
            (512, rope),
        ):
            w = w.reshape(NB * 64, -1)
            part[:, :, lo : lo + w.shape[1]] += jnp.dot(
                t, w, preferred_element_type=F32
            ).reshape(2, BLK, -1)
        return carry

    part[...] = jnp.zeros_like(part)
    lax.fori_loop(0, 4, down, 0)
    part_swap = swap(part.at[1], part_in, 5)
    part_swap.start()
    for g in ql:
        g[1].middle()
    wq_ring.middle()
    part_swap.wait_recv()
    both = part[0] + part_in[...]
    latent = both[:, :KVL]
    norm = lax.rsqrt(jnp.mean(latent * latent, axis=1, keepdims=True) + 1e-06)
    place = tab_ref[c, 4]
    lane = lax.broadcasted_iota(jnp.int32, (BLK, BLK), 1)
    rope = both[:, KVL:]
    rope = jnp.where(lane < ROPE, rope, pltpu.roll(rope, 64, 1))
    own = jnp.concatenate(
        [latent * norm * gain_ref[...], turn(rope, cos_ref[place], sin_ref[place])], axis=1
    ).astype(BF16)
    kvn_a[y, x] = own[:HALF]
    kvn_b[y, x] = own[HALF:]
    for g in kvn:
        g[0].start()
    wq_ring.end()
    wq_swap = [swap(wq.at[i, core], wq.at[i, core], 6 + i) for i in range(4)]
    for s in wq_swap:
        s.start()
    for g in kvn:
        g[0].middle()
    for g in kvn:
        g[0].end()
        g[1].start()
    for g in ql:
        g[1].end()
    for g in kvn:
        g[1].middle()
    for s in wq_swap:
        s.wait_recv()

    wide = lax.broadcasted_iota(jnp.int32, (4 * HALF, BLK), 1)

    def queries(buf, row):
        rows = slice(row, row + HALF)

        def body(i, carry):
            left = buf[i].reshape(4 * HALF, QL)
            flat = jnp.dot(left, wq[...].reshape(QL, WQ), preferred_element_type=F32)
            blocks = pl.ds(4 * i, 4)

            def put(slot, v):
                q[blocks, rows, slot * BLK : (slot + 1) * BLK] = v.astype(BF16).reshape(4, HALF, BLK)

            places = [tab_ref[4 * i + k, 4] for k in range(4)]
            cosine = jnp.concatenate([cos_ref[p, rows] for p in places], axis=0)
            sine = jnp.concatenate([sin_ref[p, rows] for p in places], axis=0)
            for j in range(HL // 2):
                one, two, three = (flat[:, k * BLK : (k + 1) * BLK] for k in range(3 * j, 3 * j + 3))
                put(2 * j, one)
                put(2 * j + 1, jnp.where(wide < 64, pltpu.roll(two, 64, 1), pltpu.roll(three, 64, 1)))
                put(HL + j, turn(jnp.where(wide < 64, two, three), cosine, sine))
            return carry

        lax.fori_loop(0, 4, body, 0)

    queries(ql_a, 0)
    queries(ql_b, HALF)
    for g in kvn:
        g[1].end()
    for s in wkv_swap:
        s.wait_recv()

    lane = lax.broadcasted_iota(jnp.int32, (4, HALF, BLK), 2)

    def keyvals(buf, row):
        rows = slice(row, row + HALF)

        def body(i, carry):
            left = buf[i]
            weight = wkv[...].reshape(KVL, WKV)
            blocks = pl.ds(3 + 4 * i, 4)
            value = jnp.dot(
                left[:, :, :KVL].reshape(4 * HALF, KVL), weight, preferred_element_type=F32
            )
            kv[blocks, rows, :] = value.astype(BF16).reshape(4, HALF, WKV)
            turned = left[:, :, KVL:].astype(F32)
            kr[blocks, rows, :BLK] = jnp.where(lane < ROPE, turned, 0.0).astype(BF16)
            kr[blocks, rows, BLK:] = jnp.where(lane < ROPE, 0.0, turned).astype(BF16)
            return carry

        lax.fori_loop(0, 4, body, 0)

    keyvals(kvn_a, 0)
    keyvals(kvn_b, HALF)

    columns = pl.ds(pl.multiple_of(c * HL * BLK, HL * BLK), HL * BLK)

    def remote(i):
        return pltpu.make_async_remote_copy(
            src_ref=obuf.at[i],
            dst_ref=o_ref.at[:, columns],
            send_sem=asem.at[i],
            recv_sem=arem.at[i],
            device_id={"ctx": shifted(c, i)},
            device_id_type=MESH,
        )

    def work(i):
        def write(h, value):
            obuf[i, :, h * BLK : (h + 1) * BLK] = value

        attend_block(shifted(c, i), tab_ref, q, kv, kr, write)

    def step(i, carry):
        work(i)
        remote(i).start()
        return carry

    lax.fori_loop(1, NB, step, 0)
    work(0)
    local = pltpu.make_async_copy(obuf.at[0], o_ref.at[:, columns], asem.at[0])
    local.start()
    for g in wd + ql + kvn + [[wq_ring, wkv_ring]]:
        for s in g:
            s.sent()
    for s in [tok_swap, part_swap] + wkv_swap + wq_swap:
        s.wait_send()
    local.wait()

    def finish(i, carry):
        remote(i).wait()
        return carry

    lax.fori_loop(1, NB, finish, 0)


def tables():
    freq = np.exp(-math.log(10000.0) * 2.0 * np.arange(32, dtype=np.float32) / ROPE).astype(np.float32)
    phase = np.arange(MOST * BLK, dtype=np.float32)[:, None] * freq[None, :]
    cosine, sine = np.cos(phase.astype(np.float64)), np.sin(phase.astype(np.float64))
    shape = (MOST, BLK, BLK)
    return (
        np.concatenate([cosine] * 4, axis=1).astype(np.float32).reshape(shape),
        np.concatenate([-sine, sine, -sine, sine], axis=1).astype(np.float32).reshape(shape),
    )


def per_device(
    tokens,
    q_latent,
    w_down_kv,
    w_down_rope,
    kv_gain,
    w_up_q,
    w_up_kv,
    lengths,
    window,
    flags,
    anchor_pick,
):
    cosine, sine = tables()
    vmem = pl.BlockSpec(memory_space=pltpu.VMEM)
    n_sem = 4 * 19
    return pl.pallas_call(
        kernel,
        name="mla",
        out_shape=jax.ShapeDtypeStruct((BLK, NB * HL * VDIM), BF16),
        in_specs=[pl.BlockSpec(memory_space=pltpu.SMEM)] * 4 + [vmem] * 9,
        out_specs=pl.BlockSpec(memory_space=pl.ANY),
        scratch_shapes=[
            pltpu.VMEM((4, 4, 4, PIECE, BLK), BF16),
            pltpu.VMEM((4, 4, 4, PIECE, BLK), BF16),
            pltpu.VMEM((4, 4, 4, PIECE, BLK), BF16),
            pltpu.VMEM((4, 4, HALF, QL), BF16),
            pltpu.VMEM((4, 4, HALF, QL), BF16),
            pltpu.VMEM((4, 4, HALF, KVR), BF16),
            pltpu.VMEM((4, 4, HALF, KVR), BF16),
            pltpu.VMEM((4, 2, QL // 8, WQ), BF16),
            pltpu.VMEM((4, 2, KVL // 8, WKV), BF16),
            pltpu.VMEM((4, 2, BLK, 8 * BLK), BF16),
            pltpu.VMEM((4, BLK, 8 * BLK), BF16),
            pltpu.VMEM((2, BLK, KVR), F32),
            pltpu.VMEM((BLK, KVR), F32),
            pltpu.VMEM((NB, BLK, WQ), BF16),
            pltpu.VMEM((NB + 3, BLK, WKV), BF16),
            pltpu.VMEM((NB + 3, BLK, 2 * BLK), BF16),
            pltpu.VMEM((NB, BLK, HL * VDIM), BF16),
            pltpu.SMEM((NB, 8), jnp.int32),
            pltpu.SemaphoreType.DMA((n_sem,)),
            pltpu.SemaphoreType.DMA((n_sem,)),
            pltpu.SemaphoreType.DMA((10,)),
            pltpu.SemaphoreType.DMA((10,)),
            pltpu.SemaphoreType.DMA((NB,)),
            pltpu.SemaphoreType.DMA((NB,)),
        ],
        compiler_params=pltpu.CompilerParams(
            collective_id=1, has_side_effects=True, vmem_limit_bytes=56 * 2**20
        ),
    )(
        lengths,
        window,
        flags,
        anchor_pick,
        tokens,
        q_latent,
        w_down_kv,
        w_down_rope,
        w_up_q,
        w_up_kv,
        kv_gain.reshape(1, KVL),
        cosine,
        sine,
    )


def solution(mesh):
    return jax.shard_map(
        per_device,
        mesh=mesh,
        in_specs=(
            P(("batch", "ctx"), None),
            P(("batch", "ctx"), None),
            P(("batch", "ctx"), None),
            P(None, ("batch", "ctx")),
            P(),
            P("batch", "ctx"),
            P("batch", "ctx"),
            P("batch", None),
            P("batch", None),
            P("batch", None),
            P("batch", None),
        ),
        out_specs=P(("batch", "ctx"), None),
        check_vma=False,
    )
```

```python
import functools
import math

import jax
import jax.numpy as jnp
import numpy as np
from jax import lax
from jax.experimental import pallas as pl
from jax.experimental.pallas import tpu as pltpu
from jax.sharding import PartitionSpec as P

NOPE = 128
ROPE = 64
VDIM = 128
BLK = 128
HALF = BLK // 2
HL = 6
NB = 16
MOST = 8
KVL = 512
QL = 1536
D = 7168
SHARD = D // 128
SPAN = NB * SHARD
WQ = HL * (NOPE + ROPE)
WKV = HL * (NOPE + VDIM)
KVR = KVL + 2 * ROPE
MESH = pl.DeviceIdType.MESH
EXP_SCALE = (NOPE + ROPE) ** (-0.5) * math.log2(math.e)
LOW = -1e30
NT = (((1,), (1,)), ((), ()))
F32 = jnp.float32
BF16 = jnp.bfloat16
ORDERS = ("xyz", "yzx", "zxy")
PIECE = 96


def shifted(c, i):
    return ((c // 4 + i // 4) % 4) * 4 + (c % 4 + i % 4) % 4


def turns(i):
    return i * 7 % NB


class Ring:
    def __init__(self, block, half, me, plus, minus, ssem, rsem, base):
        def copy(ref, device, k):
            return pltpu.make_async_remote_copy(
                src_ref=ref,
                dst_ref=ref,
                send_sem=ssem.at[base + k],
                recv_sem=rsem.at[base + k],
                device_id=device,
                device_id_type=MESH,
            )

        self.up = copy(block(me), plus, 0)
        self.down = copy(block(me), minus, 1)
        self.on_up = copy(half((me + 3) % 4, 0), plus, 2)
        self.on_down = copy(half((me + 1) % 4, 1), minus, 3)

    def start(self):
        self.up.start()
        self.down.start()

    def middle(self):
        self.up.wait_recv()
        self.on_up.start()
        self.down.wait_recv()
        self.on_down.start()

    def end(self):
        self.on_up.wait_recv()
        self.on_down.wait_recv()

    def sent(self):
        for c in (self.up, self.down, self.on_up, self.on_down):
            c.wait_send()


class Direct:
    def __init__(self, block, me, others, ssem, rsem, base):
        ref = block(me)
        self.copies = [
            pltpu.make_async_remote_copy(
                src_ref=ref,
                dst_ref=ref,
                send_sem=ssem.at[base + k],
                recv_sem=rsem.at[base + k],
                device_id=other,
                device_id_type=MESH,
            )
            for k, other in enumerate(others)
        ]

    def start(self):
        for c in self.copies:
            c.start()

    def middle(self):
        pass

    def end(self):
        for c in self.copies:
            c.wait_recv()

    def sent(self):
        for c in self.copies:
            c.wait_send()


def block_table(len_ref, window_ref, flag_ref, pick_ref, tab_ref):
    starts, anchors, start = [], [], 0
    for s in range(4):
        length, rest = len_ref[0, s], pick_ref[0, s]
        for k in range(16, -1, -1):
            rest = jnp.where(rest >= length * 2**k, rest - length * 2**k, rest)
        anchors.append(jnp.where(flag_ref[0, s] == 1, start + rest, -1))
        starts.append(start)
        start = start + length
    for t in range(NB):
        row = [0, window_ref[0, 0], anchors[0]]
        for s in range(1, 4):
            later = starts[s] <= t
            row = [
                jnp.where(later, new, old)
                for new, old in zip((starts[s], window_ref[0, s], anchors[s]), row)
            ]
        for k in range(3):
            tab_ref[t, k] = row[k]
        tab_ref[t, 3] = jnp.clip(row[2], 0, NB - 1) + 3
        tab_ref[t, 4] = jnp.clip(t - row[0], 0, MOST - 1)


def turn(v, cosine, sine):
    lane = lax.broadcasted_iota(jnp.int32, v.shape, 1)
    other = jnp.where(lane % 64 < 32, pltpu.roll(v, 96, 1), pltpu.roll(v, 32, 1))
    return v * cosine + other * sine


def attend_block(t, tab_ref, q_ref, kv_ref, kr_ref, write):
    start, window, anchor = tab_ref[t, 0], tab_ref[t, 1], tab_ref[t, 2]
    bias = []
    for j in range(4):
        kb = t - 3 + j
        ok = (kb >= start) & ((window > 3 - j) | (kb == anchor))
        bias.append(jnp.where(ok, 0.0, LOW))
    bias.append(jnp.where((anchor >= 0) & (anchor < t - 3), 0.0, LOW))
    near_blocks, far = pl.ds(t, 4), tab_ref[t, 3]
    causal = lax.broadcasted_iota(jnp.int32, (BLK, BLK), 0) >= lax.broadcasted_iota(
        jnp.int32, (BLK, BLK), 1
    )

    def score(h):
        part, column = (h % 2) * BLK, 2 * h * BLK
        query = jnp.concatenate(
            [
                q_ref[t, :, h * BLK : (h + 1) * BLK],
                q_ref[t, :, (HL + h // 2) * BLK : (HL + h // 2 + 1) * BLK],
            ],
            axis=1,
        )
        near = jnp.concatenate(
            [
                kv_ref[near_blocks, :, column : column + BLK],
                kr_ref[near_blocks, :, part : part + BLK],
            ],
            axis=2,
        ).reshape(4 * BLK, 2 * BLK)
        last = jnp.concatenate(
            [kv_ref[far, :, column : column + BLK], kr_ref[far, :, part : part + BLK]], axis=1
        )
        keys = jnp.concatenate([near, last], axis=0)
        return lax.dot_general(query, keys, NT, preferred_element_type=F32)

    def weigh(scores):
        tiles = [scores[:, j * BLK : (j + 1) * BLK] + bias[j] for j in range(5)]
        tiles[3] = jnp.where(causal, tiles[3], LOW)
        top = functools.reduce(jnp.maximum, tiles)
        top = jnp.max(top, axis=1, keepdims=True)
        weights = [jnp.exp2((tile - top) * EXP_SCALE) for tile in tiles]
        total = jnp.sum(sum(weights[1:], weights[0]), axis=1, keepdims=True)
        return jnp.concatenate([w.astype(BF16) for w in weights], axis=1), total

    def mix(h, weights, total):
        column = (2 * h + 1) * BLK
        values = jnp.concatenate(
            [
                kv_ref[near_blocks, :, column : column + BLK].reshape(4 * BLK, BLK),
                kv_ref[far, :, column : column + BLK],
            ],
            axis=0,
        )
        return jnp.dot(weights, values, preferred_element_type=F32) / total

    scores = [score(h) for h in range(HL)]
    weighed = [weigh(s) for s in scores]
    for h in range(HL):
        write(h, mix(h, *weighed[h]).astype(BF16))


def spread(tok_ref, col, store):
    lane = lax.broadcasted_iota(jnp.int32, (BLK, BLK), 1)
    for p in range(8):
        tile, off = divmod(2 * SHARD * p, BLK)
        v = tok_ref[:, pl.ds(col + tile * BLK, BLK)].astype(F32)
        if off:
            v = pltpu.roll(v, BLK - off, 1)
            if tile < 6:
                after = tok_ref[:, pl.ds(col + (tile + 1) * BLK, BLK)].astype(F32)
                v = jnp.where(lane < BLK - off, v, pltpu.roll(after, BLK - off, 1))
        store(p, jnp.where(lane < 64, v, pltpu.roll(v, 8, 1)).astype(BF16))


def kernel(
    len_ref,
    window_ref,
    flag_ref,
    pick_ref,
    tok_ref,
    ql_ref,
    wd_ref,
    wr_ref,
    wq_ref,
    wkv_ref,
    gain_ref,
    cos_ref,
    sin_ref,
    o_ref,
    wd_a,
    wd_b,
    wd_c,
    ql_a,
    ql_b,
    kvn_a,
    kvn_b,
    wq,
    wkv,
    tok,
    tok_out,
    part,
    part_in,
    q,
    kv,
    kr,
    obuf,
    tab_ref,
    ssem,
    rsem,
    csem,
    cother,
    asem,
    arem,
):
    b, c = lax.axis_index("batch"), lax.axis_index("ctx")
    z, core, y, x = b // 2, b % 2, c // 4, c % 4
    at = {"x": x, "y": y, "z": z}

    def neighbour(axis, by):
        if axis == "x":
            return {"ctx": y * 4 + (x + by) % 4}
        if axis == "y":
            return {"ctx": ((y + by) % 4) * 4 + x}
        return {"batch": ((z + by) % 4) * 2 + core}

    partner = {"batch": z * 2 + 1 - core}

    barrier = pltpu.get_barrier_semaphore()
    peers = [{"ctx": shifted(c, i)} for i in range(1, NB)]
    peers += [neighbour("z", 1), neighbour("z", 2), neighbour("z", 3), partner]
    for peer in peers:
        pl.semaphore_signal(barrier, inc=1, device_id=peer, device_id_type=MESH)

    used = [0]

    def ring(axis, block, half):
        base = used[0]
        used[0] += 4
        return Ring(
            block, half, at[axis], neighbour(axis, 1), neighbour(axis, 3), ssem, rsem, base
        )

    def direct(axis, block):
        base = used[0]
        used[0] += 4
        return Direct(block, at[axis], [neighbour(axis, k) for k in (1, 2, 3)], ssem, rsem, base)

    def gather(buf, order, mid, dims="yx", quick=0):
        stages = []
        for i, axis in enumerate(order):
            done = order[:i]

            def block(k, axis=axis, done=done):
                index = [k if a == axis else slice(None) if a in done else at[a] for a in dims]
                return buf.at[tuple(index)]

            def half(k, h, axis=axis, done=done):
                index = [k if a == axis else slice(None) if a in done else at[a] for a in dims]
                return buf.at[tuple(index) + (pl.ds(h * mid, mid),)]

            stages.append(direct(axis, block) if i < quick else ring(axis, block, half))
        return stages

    def swap(src, dst, k):
        return pltpu.make_async_remote_copy(
            src_ref=src,
            dst_ref=dst,
            send_sem=csem.at[k],
            recv_sem=cother.at[k],
            device_id=partner,
            device_id_type=MESH,
        )

    wd_buf = (wd_a, wd_b, wd_c)
    wd = [gather(buf, order, PIECE // 2, "zyx", 2) for buf, order in zip(wd_buf, ORDERS)]
    ql = [gather(ql_a, "xy", 32), gather(ql_b, "yx", 32)]
    kvn = [gather(kvn_a, "xy", 32, quick=1), gather(kvn_b, "yx", 32, quick=1)]

    def up_ring(buf, rows):
        return ring(
            "z",
            lambda k: buf.at[k, core],
            lambda k, h: buf.at[k, core, pl.ds(h * rows // 2, rows // 2)],
        )

    wq_ring, wkv_ring = up_ring(wq, QL // 8), up_ring(wkv, KVL // 8)

    down_rows = jnp.concatenate([wd_ref[...].astype(F32), jnp.zeros((64 - SHARD, KVL), F32)], axis=0)
    rope_rows = lax.dot_general(
        (
            lax.broadcasted_iota(jnp.int32, (64, SHARD), 0)
            == lax.broadcasted_iota(jnp.int32, (64, SHARD), 1)
        ).astype(F32).astype(BF16),
        jnp.concatenate([wr_ref[...], wr_ref[...]], axis=0),
        NT,
        preferred_element_type=F32,
    )
    lane = lax.broadcasted_iota(jnp.int32, (32, BLK), 1)
    pieces = (
        (down_rows[:, :128], down_rows[:32, 128:256]),
        (down_rows[:, 256:384], down_rows[32:, 128:256]),
        (down_rows[:, 384:], jnp.where(lane < 64, rope_rows[:32], rope_rows[32:])),
    )
    for buf, piece in zip(wd_buf, pieces):
        buf[z, y, x] = jnp.concatenate(piece, axis=0).astype(BF16)
    ql_a[y, x] = ql_ref[:HALF]
    ql_b[y, x] = ql_ref[HALF:]
    wkv[z, core] = wkv_ref[...]
    wq[z, core] = wq_ref[...]

    block_table(len_ref, window_ref, flag_ref, pick_ref, tab_ref)
    pl.semaphore_wait(barrier, len(peers))
    for g in wd:
        g[0].start()
    for g in ql:
        g[0].start()
    wkv_ring.start()

    def spread_out(i, carry):
        def keep(p, v):
            tok[i, 0, :, p * BLK : (p + 1) * BLK] = v

        def give(p, v):
            tok_out[i, :, p * BLK : (p + 1) * BLK] = v

        spread(tok_ref, pl.multiple_of((i * 2 + core) * SPAN, BLK), keep)
        spread(tok_ref, pl.multiple_of((i * 2 + 1 - core) * SPAN, BLK), give)
        return carry

    for g in wd:
        g[0].middle()
    lax.fori_loop(0, 4, spread_out, 0)
    tok_swap = swap(tok_out, tok.at[:, 1], 0)
    tok_swap.start()
    for g in wd:
        g[0].end()
        g[1].start()
    for g in ql:
        g[0].middle()
    for g in wd:
        g[1].middle()
    for g in wd:
        g[1].end()
        g[2].start()
    for g in ql:
        g[0].end()
        g[1].start()
    wkv_ring.middle()
    wq_ring.start()

    kv[0:3] = jnp.zeros((3, BLK, WKV), BF16)
    kr[0:3] = jnp.zeros((3, BLK, 2 * BLK), BF16)

    for g in wd:
        g[2].middle()
    wkv_ring.end()
    wkv_swap = [swap(wkv.at[i, core], wkv.at[i, core], 1 + i) for i in range(4)]
    for s in wkv_swap:
        s.start()
    tok_swap.wait_recv()
    for g in wd:
        g[2].end()

    def down(i, carry):
        t = tok[i].reshape(2 * BLK, 8 * BLK)
        first, second, third = (buf[i].reshape(NB, PIECE, BLK) for buf in wd_buf)
        shared = jnp.concatenate([first[:, 64:], second[:, 64:]], axis=1)
        packed = third[:, 64:].astype(F32)
        moved = pltpu.roll(packed.reshape(NB * 32, BLK), 64, 1).reshape(NB, 32, BLK)
        rope = jnp.concatenate([packed, moved], axis=1).astype(BF16)
        for lo, w in (
            (0, jnp.concatenate([first[:, :64], shared], axis=2)),
            (256, jnp.concatenate([second[:, :64], third[:, :64]], axis=2)),
            (512, rope),
        ):
            w = w.reshape(NB * 64, -1)
            part[:, :, lo : lo + w.shape[1]] += jnp.dot(
                t, w, preferred_element_type=F32
            ).reshape(2, BLK, -1)
        return carry

    part[...] = jnp.zeros_like(part)
    lax.fori_loop(0, 4, down, 0)
    part_swap = swap(part.at[1], part_in, 5)
    part_swap.start()
    for g in ql:
        g[1].middle()
    wq_ring.middle()
    part_swap.wait_recv()
    both = part[0] + part_in[...]
    latent = both[:, :KVL]
    norm = lax.rsqrt(jnp.mean(latent * latent, axis=1, keepdims=True) + 1e-06)
    place = tab_ref[c, 4]
    lane = lax.broadcasted_iota(jnp.int32, (BLK, BLK), 1)
    rope = both[:, KVL:]
    rope = jnp.where(lane < ROPE, rope, pltpu.roll(rope, 64, 1))
    own = jnp.concatenate(
        [latent * norm * gain_ref[...], turn(rope, cos_ref[place], sin_ref[place])], axis=1
    ).astype(BF16)
    kvn_a[y, x] = own[:HALF]
    kvn_b[y, x] = own[HALF:]
    for g in kvn:
        g[0].start()
    wq_ring.end()
    wq_swap = [swap(wq.at[i, core], wq.at[i, core], 6 + i) for i in range(4)]
    for s in wq_swap:
        s.start()
    for g in kvn:
        g[0].middle()
    for g in kvn:
        g[0].end()
        g[1].start()
    for g in ql:
        g[1].end()
    for g in kvn:
        g[1].middle()
    for s in wq_swap:
        s.wait_recv()

    wide = lax.broadcasted_iota(jnp.int32, (4 * HALF, BLK), 1)

    def queries(buf, row):
        rows = slice(row, row + HALF)

        def body(i, carry):
            left = buf[i].reshape(4 * HALF, QL)
            flat = jnp.dot(left, wq[...].reshape(QL, WQ), preferred_element_type=F32)
            blocks = pl.ds(4 * i, 4)

            def put(slot, v):
                q[blocks, rows, slot * BLK : (slot + 1) * BLK] = v.astype(BF16).reshape(4, HALF, BLK)

            places = [tab_ref[4 * i + k, 4] for k in range(4)]
            cosine = jnp.concatenate([cos_ref[p, rows] for p in places], axis=0)
            sine = jnp.concatenate([sin_ref[p, rows] for p in places], axis=0)
            for j in range(HL // 2):
                one, two, three = (flat[:, k * BLK : (k + 1) * BLK] for k in range(3 * j, 3 * j + 3))
                put(2 * j, one)
                put(2 * j + 1, jnp.where(wide < 64, pltpu.roll(two, 64, 1), pltpu.roll(three, 64, 1)))
                put(HL + j, turn(jnp.where(wide < 64, two, three), cosine, sine))
            return carry

        lax.fori_loop(0, 4, body, 0)

    queries(ql_a, 0)
    queries(ql_b, HALF)
    for g in kvn:
        g[1].end()
    for s in wkv_swap:
        s.wait_recv()

    lane = lax.broadcasted_iota(jnp.int32, (4, HALF, BLK), 2)

    def keyvals(buf, row):
        rows = slice(row, row + HALF)

        def body(i, carry):
            left = buf[i]
            weight = wkv[...].reshape(KVL, WKV)
            blocks = pl.ds(3 + 4 * i, 4)
            value = jnp.dot(
                left[:, :, :KVL].reshape(4 * HALF, KVL), weight, preferred_element_type=F32
            )
            kv[blocks, rows, :] = value.astype(BF16).reshape(4, HALF, WKV)
            turned = left[:, :, KVL:].astype(F32)
            kr[blocks, rows, :BLK] = jnp.where(lane < ROPE, turned, 0.0).astype(BF16)
            kr[blocks, rows, BLK:] = jnp.where(lane < ROPE, 0.0, turned).astype(BF16)
            return carry

        lax.fori_loop(0, 4, body, 0)

    keyvals(kvn_a, 0)
    keyvals(kvn_b, HALF)

    columns = pl.ds(pl.multiple_of(c * HL * BLK, HL * BLK), HL * BLK)

    def remote(i):
        return pltpu.make_async_remote_copy(
            src_ref=obuf.at[i],
            dst_ref=o_ref.at[:, columns],
            send_sem=asem.at[i],
            recv_sem=arem.at[i],
            device_id={"ctx": shifted(c, turns(i))},
            device_id_type=MESH,
        )

    def work(i):
        def write(h, value):
            obuf[i, :, h * BLK : (h + 1) * BLK] = value

        attend_block(shifted(c, turns(i)), tab_ref, q, kv, kr, write)

    def step(i, carry):
        work(i)
        remote(i).start()
        return carry

    lax.fori_loop(1, NB, step, 0)
    work(0)
    local = pltpu.make_async_copy(obuf.at[0], o_ref.at[:, columns], asem.at[0])
    local.start()
    for g in wd + ql + kvn + [[wq_ring, wkv_ring]]:
        for s in g:
            s.sent()
    for s in [tok_swap, part_swap] + wkv_swap + wq_swap:
        s.wait_send()
    local.wait()

    def finish(i, carry):
        remote(i).wait()
        return carry

    lax.fori_loop(1, NB, finish, 0)


def tables():
    freq = np.exp(-math.log(10000.0) * 2.0 * np.arange(32, dtype=np.float32) / ROPE).astype(np.float32)
    phase = np.arange(MOST * BLK, dtype=np.float32)[:, None] * freq[None, :]
    cosine, sine = np.cos(phase.astype(np.float64)), np.sin(phase.astype(np.float64))
    shape = (MOST, BLK, BLK)
    return (
        np.concatenate([cosine] * 4, axis=1).astype(np.float32).reshape(shape),
        np.concatenate([-sine, sine, -sine, sine], axis=1).astype(np.float32).reshape(shape),
    )


def per_device(
    tokens,
    q_latent,
    w_down_kv,
    w_down_rope,
    kv_gain,
    w_up_q,
    w_up_kv,
    lengths,
    window,
    flags,
    anchor_pick,
):
    cosine, sine = tables()
    vmem = pl.BlockSpec(memory_space=pltpu.VMEM)
    n_sem = 4 * 19
    return pl.pallas_call(
        kernel,
        name="mla",
        out_shape=pltpu.VMEM((BLK, NB * HL * VDIM), BF16),
        in_specs=[pl.BlockSpec(memory_space=pltpu.SMEM)] * 4 + [vmem] * 9,
        out_specs=pl.BlockSpec(memory_space=pltpu.VMEM),
        scratch_shapes=[
            pltpu.VMEM((4, 4, 4, PIECE, BLK), BF16),
            pltpu.VMEM((4, 4, 4, PIECE, BLK), BF16),
            pltpu.VMEM((4, 4, 4, PIECE, BLK), BF16),
            pltpu.VMEM((4, 4, HALF, QL), BF16),
            pltpu.VMEM((4, 4, HALF, QL), BF16),
            pltpu.VMEM((4, 4, HALF, KVR), BF16),
            pltpu.VMEM((4, 4, HALF, KVR), BF16),
            pltpu.VMEM((4, 2, QL // 8, WQ), BF16),
            pltpu.VMEM((4, 2, KVL // 8, WKV), BF16),
            pltpu.VMEM((4, 2, BLK, 8 * BLK), BF16),
            pltpu.VMEM((4, BLK, 8 * BLK), BF16),
            pltpu.VMEM((2, BLK, KVR), F32),
            pltpu.VMEM((BLK, KVR), F32),
            pltpu.VMEM((NB, BLK, WQ), BF16),
            pltpu.VMEM((NB + 3, BLK, WKV), BF16),
            pltpu.VMEM((NB + 3, BLK, 2 * BLK), BF16),
            pltpu.VMEM((NB, BLK, HL * VDIM), BF16),
            pltpu.SMEM((NB, 8), jnp.int32),
            pltpu.SemaphoreType.DMA((n_sem,)),
            pltpu.SemaphoreType.DMA((n_sem,)),
            pltpu.SemaphoreType.DMA((10,)),
            pltpu.SemaphoreType.DMA((10,)),
            pltpu.SemaphoreType.DMA((NB,)),
            pltpu.SemaphoreType.DMA((NB,)),
        ],
        compiler_params=pltpu.CompilerParams(
            collective_id=1, has_side_effects=True, vmem_limit_bytes=56 * 2**20
        ),
    )(
        lengths,
        window,
        flags,
        anchor_pick,
        tokens,
        q_latent,
        w_down_kv,
        w_down_rope,
        w_up_q,
        w_up_kv,
        kv_gain.reshape(1, KVL),
        cosine,
        sine,
    )


def solution(mesh):
    return jax.shard_map(
        per_device,
        mesh=mesh,
        in_specs=(
            P(("batch", "ctx"), None),
            P(("batch", "ctx"), None),
            P(("batch", "ctx"), None),
            P(None, ("batch", "ctx")),
            P(),
            P("batch", "ctx"),
            P("batch", "ctx"),
            P("batch", None),
            P("batch", None),
            P("batch", None),
            P("batch", None),
        ),
        out_specs=P(("batch", "ctx"), None),
        check_vma=False,
    )
```

```python
import functools
import math

import jax
import jax.numpy as jnp
import numpy as np
from jax import lax
from jax.experimental import pallas as pl
from jax.experimental.pallas import tpu as pltpu
from jax.sharding import PartitionSpec as P

NOPE = 128
ROPE = 64
VDIM = 128
BLK = 128
HALF = BLK // 2
HL = 6
NB = 16
MOST = 8
KVL = 512
QL = 1536
D = 7168
SHARD = D // 128
SPAN = NB * SHARD
WQ = HL * (NOPE + ROPE)
WKV = HL * (NOPE + VDIM)
KVR = KVL + 2 * ROPE
MESH = pl.DeviceIdType.MESH
EXP_SCALE = (NOPE + ROPE) ** (-0.5) * math.log2(math.e)
LOW = -1e30
NT = (((1,), (1,)), ((), ()))
F32 = jnp.float32
BF16 = jnp.bfloat16
ORDERS = ("xyz", "yzx", "zxy")
PIECE = 96


def shifted(c, i):
    return ((c // 4 + i // 4) % 4) * 4 + (c % 4 + i % 4) % 4


def turns(n):
    j = n * 2 % 9
    near = 4 * (j // 3 + j // 6) + j % 3 + (j % 3) // 2
    j = (15 - n) % 7
    a = j // 2
    a, odd = a + a // 2 - 2 * (a // 3), j % 2
    far = 4 * (2 * (1 - odd) + a * odd) + a * (1 - odd) + 2 * odd
    late = n // 9
    return near * (1 - late) + far * late


class Ring:
    def __init__(self, block, half, me, plus, minus, ssem, rsem, base):
        def copy(ref, device, k):
            return pltpu.make_async_remote_copy(
                src_ref=ref,
                dst_ref=ref,
                send_sem=ssem.at[base + k],
                recv_sem=rsem.at[base + k],
                device_id=device,
                device_id_type=MESH,
            )

        self.up = copy(block(me), plus, 0)
        self.down = copy(block(me), minus, 1)
        self.on_up = copy(half((me + 3) % 4, 0), plus, 2)
        self.on_down = copy(half((me + 1) % 4, 1), minus, 3)

    def start(self):
        self.up.start()
        self.down.start()

    def middle(self):
        self.up.wait_recv()
        self.on_up.start()
        self.down.wait_recv()
        self.on_down.start()

    def end(self):
        self.on_up.wait_recv()
        self.on_down.wait_recv()

    def sent(self):
        for c in (self.up, self.down, self.on_up, self.on_down):
            c.wait_send()


class Direct:
    def __init__(self, block, me, others, ssem, rsem, base):
        ref = block(me)
        self.copies = [
            pltpu.make_async_remote_copy(
                src_ref=ref,
                dst_ref=ref,
                send_sem=ssem.at[base + k],
                recv_sem=rsem.at[base + k],
                device_id=other,
                device_id_type=MESH,
            )
            for k, other in enumerate(others)
        ]

    def start(self):
        for c in self.copies:
            c.start()

    def middle(self):
        pass

    def end(self):
        for c in self.copies:
            c.wait_recv()

    def sent(self):
        for c in self.copies:
            c.wait_send()


def block_table(len_ref, window_ref, flag_ref, pick_ref, tab_ref):
    starts, anchors, start = [], [], 0
    for s in range(4):
        length, rest = len_ref[0, s], pick_ref[0, s]
        for k in range(16, -1, -1):
            rest = jnp.where(rest >= length * 2**k, rest - length * 2**k, rest)
        anchors.append(jnp.where(flag_ref[0, s] == 1, start + rest, -1))
        starts.append(start)
        start = start + length
    for t in range(NB):
        row = [0, window_ref[0, 0], anchors[0]]
        for s in range(1, 4):
            later = starts[s] <= t
            row = [
                jnp.where(later, new, old)
                for new, old in zip((starts[s], window_ref[0, s], anchors[s]), row)
            ]
        for k in range(3):
            tab_ref[t, k] = row[k]
        tab_ref[t, 3] = jnp.clip(row[2], 0, NB - 1) + 3
        tab_ref[t, 4] = jnp.clip(t - row[0], 0, MOST - 1)


def turn(v, cosine, sine):
    lane = lax.broadcasted_iota(jnp.int32, v.shape, 1)
    other = jnp.where(lane % 64 < 32, pltpu.roll(v, 96, 1), pltpu.roll(v, 32, 1))
    return v * cosine + other * sine


def attend_block(t, tab_ref, q_ref, kv_ref, kr_ref, write):
    start, window, anchor = tab_ref[t, 0], tab_ref[t, 1], tab_ref[t, 2]
    bias = []
    for j in range(4):
        kb = t - 3 + j
        ok = (kb >= start) & ((window > 3 - j) | (kb == anchor))
        bias.append(jnp.where(ok, 0.0, LOW))
    bias.append(jnp.where((anchor >= 0) & (anchor < t - 3), 0.0, LOW))
    near_blocks, far = pl.ds(t, 4), tab_ref[t, 3]
    causal = lax.broadcasted_iota(jnp.int32, (BLK, BLK), 0) >= lax.broadcasted_iota(
        jnp.int32, (BLK, BLK), 1
    )

    def score(h):
        part, column = (h % 2) * BLK, 2 * h * BLK
        query = jnp.concatenate(
            [
                q_ref[t, :, h * BLK : (h + 1) * BLK],
                q_ref[t, :, (HL + h // 2) * BLK : (HL + h // 2 + 1) * BLK],
            ],
            axis=1,
        )
        near = jnp.concatenate(
            [
                kv_ref[near_blocks, :, column : column + BLK],
                kr_ref[near_blocks, :, part : part + BLK],
            ],
            axis=2,
        ).reshape(4 * BLK, 2 * BLK)
        last = jnp.concatenate(
            [kv_ref[far, :, column : column + BLK], kr_ref[far, :, part : part + BLK]], axis=1
        )
        keys = jnp.concatenate([near, last], axis=0)
        return lax.dot_general(query, keys, NT, preferred_element_type=F32)

    def weigh(scores):
        tiles = [scores[:, j * BLK : (j + 1) * BLK] + bias[j] for j in range(5)]
        tiles[3] = jnp.where(causal, tiles[3], LOW)
        top = functools.reduce(jnp.maximum, tiles)
        top = jnp.max(top, axis=1, keepdims=True)
        weights = [jnp.exp2((tile - top) * EXP_SCALE) for tile in tiles]
        total = jnp.sum(sum(weights[1:], weights[0]), axis=1, keepdims=True)
        return jnp.concatenate([w.astype(BF16) for w in weights], axis=1), total

    def mix(h, weights, total):
        column = (2 * h + 1) * BLK
        values = jnp.concatenate(
            [
                kv_ref[near_blocks, :, column : column + BLK].reshape(4 * BLK, BLK),
                kv_ref[far, :, column : column + BLK],
            ],
            axis=0,
        )
        return jnp.dot(weights, values, preferred_element_type=F32) / total

    scores = [score(h) for h in range(HL)]
    weighed = [weigh(s) for s in scores]
    for h in range(HL):
        write(h, mix(h, *weighed[h]).astype(BF16))


def spread(tok_ref, col, store):
    lane = lax.broadcasted_iota(jnp.int32, (BLK, BLK), 1)
    for p in range(8):
        tile, off = divmod(2 * SHARD * p, BLK)
        v = tok_ref[:, pl.ds(col + tile * BLK, BLK)].astype(F32)
        if off:
            v = pltpu.roll(v, BLK - off, 1)
            if tile < 6:
                after = tok_ref[:, pl.ds(col + (tile + 1) * BLK, BLK)].astype(F32)
                v = jnp.where(lane < BLK - off, v, pltpu.roll(after, BLK - off, 1))
        store(p, jnp.where(lane < 64, v, pltpu.roll(v, 8, 1)).astype(BF16))


def kernel(
    len_ref,
    window_ref,
    flag_ref,
    pick_ref,
    tok_ref,
    ql_ref,
    wd_ref,
    wr_ref,
    wq_ref,
    wkv_ref,
    gain_ref,
    cos_ref,
    sin_ref,
    o_ref,
    wd_a,
    wd_b,
    wd_c,
    ql_a,
    ql_b,
    kvn_a,
    kvn_b,
    wq,
    wkv,
    tok,
    tok_out,
    part,
    part_in,
    q,
    kv,
    kr,
    obuf,
    tab_ref,
    ssem,
    rsem,
    csem,
    cother,
    asem,
    arem,
):
    b, c = lax.axis_index("batch"), lax.axis_index("ctx")
    z, core, y, x = b // 2, b % 2, c // 4, c % 4
    at = {"x": x, "y": y, "z": z}

    def neighbour(axis, by):
        if axis == "x":
            return {"ctx": y * 4 + (x + by) % 4}
        if axis == "y":
            return {"ctx": ((y + by) % 4) * 4 + x}
        return {"batch": ((z + by) % 4) * 2 + core}

    partner = {"batch": z * 2 + 1 - core}

    barrier = pltpu.get_barrier_semaphore()
    peers = [{"ctx": shifted(c, i)} for i in range(1, NB)]
    peers += [neighbour("z", 1), neighbour("z", 2), neighbour("z", 3), partner]
    for peer in peers:
        pl.semaphore_signal(barrier, inc=1, device_id=peer, device_id_type=MESH)

    used = [0]

    def ring(axis, block, half):
        base = used[0]
        used[0] += 4
        return Ring(
            block, half, at[axis], neighbour(axis, 1), neighbour(axis, 3), ssem, rsem, base
        )

    def direct(axis, block):
        base = used[0]
        used[0] += 4
        return Direct(block, at[axis], [neighbour(axis, k) for k in (1, 2, 3)], ssem, rsem, base)

    def gather(buf, order, mid, dims="yx", quick=0):
        stages = []
        for i, axis in enumerate(order):
            done = order[:i]

            def block(k, axis=axis, done=done):
                index = [k if a == axis else slice(None) if a in done else at[a] for a in dims]
                return buf.at[tuple(index)]

            def half(k, h, axis=axis, done=done):
                index = [k if a == axis else slice(None) if a in done else at[a] for a in dims]
                return buf.at[tuple(index) + (pl.ds(h * mid, mid),)]

            stages.append(direct(axis, block) if i < quick else ring(axis, block, half))
        return stages

    def swap(src, dst, k):
        return pltpu.make_async_remote_copy(
            src_ref=src,
            dst_ref=dst,
            send_sem=csem.at[k],
            recv_sem=cother.at[k],
            device_id=partner,
            device_id_type=MESH,
        )

    wd_buf = (wd_a, wd_b, wd_c)
    wd = [gather(buf, order, PIECE // 2, "zyx", 2) for buf, order in zip(wd_buf, ORDERS)]
    ql = [gather(ql_a, "xy", 32), gather(ql_b, "yx", 32)]
    kvn = [gather(kvn_a, "xy", 32, quick=1), gather(kvn_b, "yx", 32, quick=1)]

    def up_ring(buf, rows):
        return ring(
            "z",
            lambda k: buf.at[k, core],
            lambda k, h: buf.at[k, core, pl.ds(h * rows // 2, rows // 2)],
        )

    wq_ring, wkv_ring = up_ring(wq, QL // 8), up_ring(wkv, KVL // 8)

    down_rows = jnp.concatenate([wd_ref[...].astype(F32), jnp.zeros((64 - SHARD, KVL), F32)], axis=0)
    rope_rows = lax.dot_general(
        (
            lax.broadcasted_iota(jnp.int32, (64, SHARD), 0)
            == lax.broadcasted_iota(jnp.int32, (64, SHARD), 1)
        ).astype(F32).astype(BF16),
        jnp.concatenate([wr_ref[...], wr_ref[...]], axis=0),
        NT,
        preferred_element_type=F32,
    )
    lane = lax.broadcasted_iota(jnp.int32, (32, BLK), 1)
    pieces = (
        (down_rows[:, :128], down_rows[:32, 128:256]),
        (down_rows[:, 256:384], down_rows[32:, 128:256]),
        (down_rows[:, 384:], jnp.where(lane < 64, rope_rows[:32], rope_rows[32:])),
    )
    for buf, piece in zip(wd_buf, pieces):
        buf[z, y, x] = jnp.concatenate(piece, axis=0).astype(BF16)
    ql_a[y, x] = ql_ref[:HALF]
    ql_b[y, x] = ql_ref[HALF:]
    wkv[z, core] = wkv_ref[...]
    wq[z, core] = wq_ref[...]

    block_table(len_ref, window_ref, flag_ref, pick_ref, tab_ref)
    pl.semaphore_wait(barrier, len(peers))
    for g in wd:
        g[0].start()
    for g in ql:
        g[0].start()
    wkv_ring.start()

    def spread_out(i, carry):
        def keep(p, v):
            tok[i, 0, :, p * BLK : (p + 1) * BLK] = v

        def give(p, v):
            tok_out[i, :, p * BLK : (p + 1) * BLK] = v

        spread(tok_ref, pl.multiple_of((i * 2 + core) * SPAN, BLK), keep)
        spread(tok_ref, pl.multiple_of((i * 2 + 1 - core) * SPAN, BLK), give)
        return carry

    for g in wd:
        g[0].middle()
    lax.fori_loop(0, 4, spread_out, 0)
    tok_swap = swap(tok_out, tok.at[:, 1], 0)
    tok_swap.start()
    for g in wd:
        g[0].end()
        g[1].start()
    for g in ql:
        g[0].middle()
    for g in wd:
        g[1].middle()
    for g in wd:
        g[1].end()
        g[2].start()
    wkv_ring.middle()

    kv[0:3] = jnp.zeros((3, BLK, WKV), BF16)
    kr[0:3] = jnp.zeros((3, BLK, 2 * BLK), BF16)

    for g in wd:
        g[2].middle()
    for g in ql:
        g[0].end()
        g[1].start()
    wq_ring.start()
    wkv_ring.end()
    wkv_swap = [swap(wkv.at[i, core], wkv.at[i, core], 1 + i) for i in range(4)]
    for s in wkv_swap:
        s.start()
    tok_swap.wait_recv()
    for g in wd:
        g[2].end()

    def down(i, carry):
        t = tok[i].reshape(2 * BLK, 8 * BLK)
        first, second, third = (buf[i].reshape(NB, PIECE, BLK) for buf in wd_buf)
        shared = jnp.concatenate([first[:, 64:], second[:, 64:]], axis=1)
        packed = third[:, 64:].astype(F32)
        moved = pltpu.roll(packed.reshape(NB * 32, BLK), 64, 1).reshape(NB, 32, BLK)
        rope = jnp.concatenate([packed, moved], axis=1).astype(BF16)
        for lo, w in (
            (0, jnp.concatenate([first[:, :64], shared], axis=2)),
            (256, jnp.concatenate([second[:, :64], third[:, :64]], axis=2)),
            (512, rope),
        ):
            w = w.reshape(NB * 64, -1)
            part[:, :, lo : lo + w.shape[1]] += jnp.dot(
                t, w, preferred_element_type=F32
            ).reshape(2, BLK, -1)
        return carry

    part[...] = jnp.zeros_like(part)
    lax.fori_loop(0, 4, down, 0)
    part_swap = swap(part.at[1], part_in, 5)
    part_swap.start()
    part_swap.wait_recv()
    both = part[0] + part_in[...]
    latent = both[:, :KVL]
    norm = lax.rsqrt(jnp.mean(latent * latent, axis=1, keepdims=True) + 1e-06)
    place = tab_ref[c, 4]
    lane = lax.broadcasted_iota(jnp.int32, (BLK, BLK), 1)
    rope = both[:, KVL:]
    rope = jnp.where(lane < ROPE, rope, pltpu.roll(rope, 64, 1))
    own = jnp.concatenate(
        [latent * norm * gain_ref[...], turn(rope, cos_ref[place], sin_ref[place])], axis=1
    ).astype(BF16)
    kvn_a[y, x] = own[:HALF]
    kvn_b[y, x] = own[HALF:]
    for g in kvn:
        g[0].start()
    for g in kvn:
        g[0].end()
        g[1].start()
    for g in ql:
        g[1].middle()
    wq_ring.middle()
    wq_ring.end()
    wq_swap = [swap(wq.at[i, core], wq.at[i, core], 6 + i) for i in range(4)]
    for s in wq_swap:
        s.start()

    def arrival(me, j):
        return (me + j + j // 2 - 2 * (j // 3)) % 4

    wide = lax.broadcasted_iota(jnp.int32, (4 * HALF, BLK), 1)

    def line(along, j):
        if along == "y":
            return [(arrival(y, j), k) for k in range(4)]
        return [(k, arrival(x, j)) for k in range(4)]

    def queries(buf, row, along, first, last):
        rows = slice(row, row + HALF)

        def body(j, carry):
            places = line(along, j)
            left = jnp.concatenate([buf[p] for p in places], axis=0)
            places = [4 * yy + xx for yy, xx in places]
            flat = jnp.dot(left, wq[...].reshape(QL, WQ), preferred_element_type=F32)

            def put(slot, v):
                v = v.astype(BF16)
                for k, t in enumerate(places):
                    q[t, rows, slot * BLK : (slot + 1) * BLK] = v[k * HALF : (k + 1) * HALF]

            turns_of = [tab_ref[t, 4] for t in places]
            cosine = jnp.concatenate([cos_ref[p, rows] for p in turns_of], axis=0)
            sine = jnp.concatenate([sin_ref[p, rows] for p in turns_of], axis=0)
            for j in range(HL // 2):
                one, two, three = (flat[:, k * BLK : (k + 1) * BLK] for k in range(3 * j, 3 * j + 3))
                put(2 * j, one)
                put(2 * j + 1, jnp.where(wide < 64, pltpu.roll(two, 64, 1), pltpu.roll(three, 64, 1)))
                put(HL + j, turn(jnp.where(wide < 64, two, three), cosine, sine))
            return carry

        lax.fori_loop(first, last, body, 0)

    lane = lax.broadcasted_iota(jnp.int32, (HALF, BLK), 1)

    def keyvals(buf, row, along, first, last):
        rows = slice(row, row + HALF)

        def body(j, carry):
            places = line(along, j)
            left = [buf[p] for p in places]
            value = jnp.dot(
                jnp.concatenate([v[:, :KVL] for v in left], axis=0),
                wkv[...].reshape(KVL, WKV),
                preferred_element_type=F32,
            ).astype(BF16)
            for k, (yy, xx) in enumerate(places):
                t = 3 + 4 * yy + xx
                kv[t, rows, :] = value[k * HALF : (k + 1) * HALF]
                turned = left[k][:, KVL:].astype(F32)
                kr[t, rows, :BLK] = jnp.where(lane < ROPE, turned, 0.0).astype(BF16)
                kr[t, rows, BLK:] = jnp.where(lane < ROPE, 0.0, turned).astype(BF16)
            return carry

        lax.fori_loop(first, last, body, 0)

    for g in kvn:
        g[1].middle()
    for s in wkv_swap:
        s.wait_recv()
    keyvals(kvn_a, 0, "y", 0, 3)
    keyvals(kvn_b, HALF, "x", 0, 3)
    for s in wq_swap:
        s.wait_recv()
    queries(ql_a, 0, "y", 0, 3)
    queries(ql_b, HALF, "x", 0, 3)
    for g in kvn:
        g[1].end()
    keyvals(kvn_a, 0, "y", 3, 4)
    keyvals(kvn_b, HALF, "x", 3, 4)

    columns = pl.ds(pl.multiple_of(c * HL * BLK, HL * BLK), HL * BLK)

    def remote(i):
        return pltpu.make_async_remote_copy(
            src_ref=obuf.at[i],
            dst_ref=o_ref.at[:, columns],
            send_sem=asem.at[i],
            recv_sem=arem.at[i],
            device_id={"ctx": shifted(c, turns(i))},
            device_id_type=MESH,
        )

    def work(i):
        def write(h, value):
            obuf[i, :, h * BLK : (h + 1) * BLK] = value

        attend_block(shifted(c, turns(i)), tab_ref, q, kv, kr, write)

    def step(i, carry):
        @pl.when(i == 9)
        def _():
            for g in ql:
                g[1].end()
            queries(ql_a, 0, "y", 3, 4)
            queries(ql_b, HALF, "x", 3, 4)

        work(i)
        remote(i).start()
        return carry

    lax.fori_loop(1, NB, step, 0)
    work(0)
    local = pltpu.make_async_copy(obuf.at[0], o_ref.at[:, columns], asem.at[0])
    local.start()
    for g in wd + ql + kvn + [[wq_ring, wkv_ring]]:
        for s in g:
            s.sent()
    for s in [tok_swap, part_swap] + wkv_swap + wq_swap:
        s.wait_send()
    local.wait()

    def finish(i, carry):
        remote(i).wait()
        return carry

    lax.fori_loop(1, NB, finish, 0)


def tables():
    freq = np.exp(-math.log(10000.0) * 2.0 * np.arange(32, dtype=np.float32) / ROPE).astype(np.float32)
    phase = np.arange(MOST * BLK, dtype=np.float32)[:, None] * freq[None, :]
    cosine, sine = np.cos(phase.astype(np.float64)), np.sin(phase.astype(np.float64))
    shape = (MOST, BLK, BLK)
    return (
        np.concatenate([cosine] * 4, axis=1).astype(np.float32).reshape(shape),
        np.concatenate([-sine, sine, -sine, sine], axis=1).astype(np.float32).reshape(shape),
    )


def per_device(
    tokens,
    q_latent,
    w_down_kv,
    w_down_rope,
    kv_gain,
    w_up_q,
    w_up_kv,
    lengths,
    window,
    flags,
    anchor_pick,
):
    cosine, sine = tables()
    vmem = pl.BlockSpec(memory_space=pltpu.VMEM)
    n_sem = 4 * 19
    return pl.pallas_call(
        kernel,
        name="mla",
        out_shape=pltpu.VMEM((BLK, NB * HL * VDIM), BF16),
        in_specs=[pl.BlockSpec(memory_space=pltpu.SMEM)] * 4 + [vmem] * 9,
        out_specs=pl.BlockSpec(memory_space=pltpu.VMEM),
        scratch_shapes=[
            pltpu.VMEM((4, 4, 4, PIECE, BLK), BF16),
            pltpu.VMEM((4, 4, 4, PIECE, BLK), BF16),
            pltpu.VMEM((4, 4, 4, PIECE, BLK), BF16),
            pltpu.VMEM((4, 4, HALF, QL), BF16),
            pltpu.VMEM((4, 4, HALF, QL), BF16),
            pltpu.VMEM((4, 4, HALF, KVR), BF16),
            pltpu.VMEM((4, 4, HALF, KVR), BF16),
            pltpu.VMEM((4, 2, QL // 8, WQ), BF16),
            pltpu.VMEM((4, 2, KVL // 8, WKV), BF16),
            pltpu.VMEM((4, 2, BLK, 8 * BLK), BF16),
            pltpu.VMEM((4, BLK, 8 * BLK), BF16),
            pltpu.VMEM((2, BLK, KVR), F32),
            pltpu.VMEM((BLK, KVR), F32),
            pltpu.VMEM((NB, BLK, WQ), BF16),
            pltpu.VMEM((NB + 3, BLK, WKV), BF16),
            pltpu.VMEM((NB + 3, BLK, 2 * BLK), BF16),
            pltpu.VMEM((NB, BLK, HL * VDIM), BF16),
            pltpu.SMEM((NB, 8), jnp.int32),
            pltpu.SemaphoreType.DMA((n_sem,)),
            pltpu.SemaphoreType.DMA((n_sem,)),
            pltpu.SemaphoreType.DMA((10,)),
            pltpu.SemaphoreType.DMA((10,)),
            pltpu.SemaphoreType.DMA((NB,)),
            pltpu.SemaphoreType.DMA((NB,)),
        ],
        compiler_params=pltpu.CompilerParams(
            collective_id=1, has_side_effects=True, vmem_limit_bytes=56 * 2**20
        ),
    )(
        lengths,
        window,
        flags,
        anchor_pick,
        tokens,
        q_latent,
        w_down_kv,
        w_down_rope,
        w_up_q,
        w_up_kv,
        kv_gain.reshape(1, KVL),
        cosine,
        sine,
    )


def solution(mesh):
    return jax.shard_map(
        per_device,
        mesh=mesh,
        in_specs=(
            P(("batch", "ctx"), None),
            P(("batch", "ctx"), None),
            P(("batch", "ctx"), None),
            P(None, ("batch", "ctx")),
            P(),
            P("batch", "ctx"),
            P("batch", "ctx"),
            P("batch", None),
            P("batch", None),
            P("batch", None),
            P("batch", None),
        ),
        out_specs=P(("batch", "ctx"), None),
        check_vma=False,
    )
```

```python
import functools
import math

import jax
import jax.numpy as jnp
import numpy as np
from jax import lax
from jax.experimental import pallas as pl
from jax.experimental.pallas import tpu as pltpu
from jax.sharding import PartitionSpec as P

NOPE = 128
ROPE = 64
VDIM = 128
BLK = 128
HALF = BLK // 2
HL = 6
NB = 16
MOST = 8
KVL = 512
QL = 1536
D = 7168
SHARD = D // 128
SPAN = NB * SHARD
WQ = HL * (NOPE + ROPE)
WKV = HL * (NOPE + VDIM)
KVR = KVL + 2 * ROPE
MESH = pl.DeviceIdType.MESH
EXP_SCALE = (NOPE + ROPE) ** (-0.5) * math.log2(math.e)
LOW = -1e30
NT = (((1,), (1,)), ((), ()))
F32 = jnp.float32
BF16 = jnp.bfloat16
ORDERS = ("xyz", "yzx", "zxy")
PIECE = 96


def shifted(c, i):
    return ((c // 4 + i // 4) % 4) * 4 + (c % 4 + i % 4) % 4


def turns(n):
    j = n * 4 % 9
    near = 4 * (j // 3 + j // 6) + j % 3 + (j % 3) // 2
    j = (15 - n) % 7
    a = j // 2
    a, odd = a + a // 2 - 2 * (a // 3), j % 2
    far = 4 * (2 * (1 - odd) + a * odd) + a * (1 - odd) + 2 * odd
    late = n // 9
    return near * (1 - late) + far * late


class Ring:
    def __init__(self, block, half, me, plus, minus, ssem, rsem, base):
        def copy(ref, device, k):
            return pltpu.make_async_remote_copy(
                src_ref=ref,
                dst_ref=ref,
                send_sem=ssem.at[base + k],
                recv_sem=rsem.at[base + k],
                device_id=device,
                device_id_type=MESH,
            )

        self.up = copy(block(me), plus, 0)
        self.down = copy(block(me), minus, 1)
        self.on_up = copy(half((me + 3) % 4, 0), plus, 2)
        self.on_down = copy(half((me + 1) % 4, 1), minus, 3)

    def start(self):
        self.up.start()
        self.down.start()

    def middle(self):
        self.up.wait_recv()
        self.on_up.start()
        self.down.wait_recv()
        self.on_down.start()

    def end(self):
        self.on_up.wait_recv()
        self.on_down.wait_recv()

    def sent(self):
        for c in (self.up, self.down, self.on_up, self.on_down):
            c.wait_send()


class Direct:
    def __init__(self, block, me, others, ssem, rsem, base):
        ref = block(me)
        self.copies = [
            pltpu.make_async_remote_copy(
                src_ref=ref,
                dst_ref=ref,
                send_sem=ssem.at[base + k],
                recv_sem=rsem.at[base + k],
                device_id=other,
                device_id_type=MESH,
            )
            for k, other in enumerate(others)
        ]

    def start(self):
        for c in self.copies:
            c.start()

    def middle(self):
        pass

    def end(self):
        for c in self.copies:
            c.wait_recv()

    def sent(self):
        for c in self.copies:
            c.wait_send()


def block_table(len_ref, window_ref, flag_ref, pick_ref, tab_ref):
    starts, anchors, start = [], [], 0
    for s in range(4):
        length, rest = len_ref[0, s], pick_ref[0, s]
        for k in range(16, -1, -1):
            rest = jnp.where(rest >= length * 2**k, rest - length * 2**k, rest)
        anchors.append(jnp.where(flag_ref[0, s] == 1, start + rest, -1))
        starts.append(start)
        start = start + length
    for t in range(NB):
        row = [0, window_ref[0, 0], anchors[0]]
        for s in range(1, 4):
            later = starts[s] <= t
            row = [
                jnp.where(later, new, old)
                for new, old in zip((starts[s], window_ref[0, s], anchors[s]), row)
            ]
        for k in range(3):
            tab_ref[t, k] = row[k]
        tab_ref[t, 3] = jnp.clip(row[2], 0, NB - 1) + 3
        tab_ref[t, 4] = jnp.clip(t - row[0], 0, MOST - 1)


def turn(v, cosine, sine):
    lane = lax.broadcasted_iota(jnp.int32, v.shape, 1)
    other = jnp.where(lane % 64 < 32, pltpu.roll(v, 96, 1), pltpu.roll(v, 32, 1))
    return v * cosine + other * sine


def attend_block(t, tab_ref, q_ref, kv_ref, kr_ref, write):
    start, window, anchor = tab_ref[t, 0], tab_ref[t, 1], tab_ref[t, 2]
    bias = []
    for j in range(4):
        kb = t - 3 + j
        ok = (kb >= start) & ((window > 3 - j) | (kb == anchor))
        bias.append(jnp.where(ok, 0.0, LOW))
    bias.append(jnp.where((anchor >= 0) & (anchor < t - 3), 0.0, LOW))
    near_blocks, far = pl.ds(t, 4), tab_ref[t, 3]
    causal = lax.broadcasted_iota(jnp.int32, (BLK, BLK), 0) >= lax.broadcasted_iota(
        jnp.int32, (BLK, BLK), 1
    )

    def score(h):
        part, column = (h % 2) * BLK, 2 * h * BLK
        query = jnp.concatenate(
            [
                q_ref[t, :, h * BLK : (h + 1) * BLK],
                q_ref[t, :, (HL + h // 2) * BLK : (HL + h // 2 + 1) * BLK],
            ],
            axis=1,
        )
        near = jnp.concatenate(
            [
                kv_ref[near_blocks, :, column : column + BLK],
                kr_ref[near_blocks, :, part : part + BLK],
            ],
            axis=2,
        ).reshape(4 * BLK, 2 * BLK)
        last = jnp.concatenate(
            [kv_ref[far, :, column : column + BLK], kr_ref[far, :, part : part + BLK]], axis=1
        )
        keys = jnp.concatenate([near, last], axis=0)
        return lax.dot_general(query, keys, NT, preferred_element_type=F32)

    def weigh(scores):
        tiles = [scores[:, j * BLK : (j + 1) * BLK] + bias[j] for j in range(5)]
        tiles[3] = jnp.where(causal, tiles[3], LOW)
        top = functools.reduce(jnp.maximum, tiles)
        top = jnp.max(top, axis=1, keepdims=True)
        weights = [jnp.exp2((tile - top) * EXP_SCALE) for tile in tiles]
        total = jnp.sum(sum(weights[1:], weights[0]), axis=1, keepdims=True)
        return jnp.concatenate([w.astype(BF16) for w in weights], axis=1), total

    def mix(h, weights, total):
        column = (2 * h + 1) * BLK
        values = jnp.concatenate(
            [
                kv_ref[near_blocks, :, column : column + BLK].reshape(4 * BLK, BLK),
                kv_ref[far, :, column : column + BLK],
            ],
            axis=0,
        )
        return jnp.dot(weights, values, preferred_element_type=F32) / total

    scores = [score(h) for h in range(HL)]
    weighed = [weigh(s) for s in scores]
    for h in range(HL):
        write(h, mix(h, *weighed[h]).astype(BF16))


def spread(tok_ref, col, store):
    lane = lax.broadcasted_iota(jnp.int32, (BLK, BLK), 1)
    for p in range(8):
        tile, off = divmod(2 * SHARD * p, BLK)
        v = tok_ref[:, pl.ds(col + tile * BLK, BLK)].astype(F32)
        if off:
            v = pltpu.roll(v, BLK - off, 1)
            if tile < 6:
                after = tok_ref[:, pl.ds(col + (tile + 1) * BLK, BLK)].astype(F32)
                v = jnp.where(lane < BLK - off, v, pltpu.roll(after, BLK - off, 1))
        store(p, jnp.where(lane < 64, v, pltpu.roll(v, 8, 1)).astype(BF16))


def kernel(
    len_ref,
    window_ref,
    flag_ref,
    pick_ref,
    tok_ref,
    ql_ref,
    wd_ref,
    wr_ref,
    wq_ref,
    wkv_ref,
    gain_ref,
    cos_ref,
    sin_ref,
    o_ref,
    wd_a,
    wd_b,
    wd_c,
    ql_a,
    ql_b,
    kvn_a,
    kvn_b,
    wq,
    wkv,
    tok,
    tok_out,
    part,
    part_in,
    q,
    kv,
    kr,
    obuf,
    tab_ref,
    ssem,
    rsem,
    csem,
    cother,
    asem,
    arem,
):
    b, c = lax.axis_index("batch"), lax.axis_index("ctx")
    z, core, y, x = b // 2, b % 2, c // 4, c % 4
    at = {"x": x, "y": y, "z": z}

    def neighbour(axis, by):
        if axis == "x":
            return {"ctx": y * 4 + (x + by) % 4}
        if axis == "y":
            return {"ctx": ((y + by) % 4) * 4 + x}
        return {"batch": ((z + by) % 4) * 2 + core}

    partner = {"batch": z * 2 + 1 - core}

    barrier = pltpu.get_barrier_semaphore()
    peers = [{"ctx": shifted(c, i)} for i in range(1, NB)]
    peers += [neighbour("z", 1), neighbour("z", 2), neighbour("z", 3), partner]
    for peer in peers:
        pl.semaphore_signal(barrier, inc=1, device_id=peer, device_id_type=MESH)

    used = [0]

    def ring(axis, block, half):
        base = used[0]
        used[0] += 4
        return Ring(
            block, half, at[axis], neighbour(axis, 1), neighbour(axis, 3), ssem, rsem, base
        )

    def direct(axis, block):
        base = used[0]
        used[0] += 4
        return Direct(block, at[axis], [neighbour(axis, k) for k in (1, 2, 3)], ssem, rsem, base)

    def gather(buf, order, mid, dims="yx", quick=0):
        stages = []
        for i, axis in enumerate(order):
            done = order[:i]

            def block(k, axis=axis, done=done):
                index = [k if a == axis else slice(None) if a in done else at[a] for a in dims]
                return buf.at[tuple(index)]

            def half(k, h, axis=axis, done=done):
                index = [k if a == axis else slice(None) if a in done else at[a] for a in dims]
                return buf.at[tuple(index) + (pl.ds(h * mid, mid),)]

            stages.append(direct(axis, block) if i < quick else ring(axis, block, half))
        return stages

    def swap(src, dst, k):
        return pltpu.make_async_remote_copy(
            src_ref=src,
            dst_ref=dst,
            send_sem=csem.at[k],
            recv_sem=cother.at[k],
            device_id=partner,
            device_id_type=MESH,
        )

    wd_buf = (wd_a, wd_b, wd_c)
    wd = [gather(buf, order, PIECE // 2, "zyx", 2) for buf, order in zip(wd_buf, ORDERS)]
    ql = [gather(ql_a, "xy", 32), gather(ql_b, "yx", 32)]
    kvn = [gather(kvn_a, "xy", 32, quick=1), gather(kvn_b, "yx", 32, quick=1)]

    def up_ring(buf, rows):
        return ring(
            "z",
            lambda k: buf.at[k, core],
            lambda k, h: buf.at[k, core, pl.ds(h * rows // 2, rows // 2)],
        )

    wq_ring, wkv_ring = up_ring(wq, QL // 8), up_ring(wkv, KVL // 8)

    down_rows = jnp.concatenate([wd_ref[...].astype(F32), jnp.zeros((64 - SHARD, KVL), F32)], axis=0)
    rope_rows = lax.dot_general(
        (
            lax.broadcasted_iota(jnp.int32, (64, SHARD), 0)
            == lax.broadcasted_iota(jnp.int32, (64, SHARD), 1)
        ).astype(F32).astype(BF16),
        jnp.concatenate([wr_ref[...], wr_ref[...]], axis=0),
        NT,
        preferred_element_type=F32,
    )
    lane = lax.broadcasted_iota(jnp.int32, (32, BLK), 1)
    pieces = (
        (down_rows[:, :128], down_rows[:32, 128:256]),
        (down_rows[:, 256:384], down_rows[32:, 128:256]),
        (down_rows[:, 384:], jnp.where(lane < 64, rope_rows[:32], rope_rows[32:])),
    )
    for buf, piece in zip(wd_buf, pieces):
        buf[z, y, x] = jnp.concatenate(piece, axis=0).astype(BF16)

    pl.semaphore_wait(barrier, len(peers))
    for g in wd:
        g[0].start()
    ql_a[y, x] = ql_ref[:HALF]
    ql_b[y, x] = ql_ref[HALF:]
    for g in ql:
        g[0].start()
    for g in wd:
        g[0].end()
        g[1].start()
    wkv[z, core] = wkv_ref[...]
    wq[z, core] = wq_ref[...]
    for g in ql:
        g[0].middle()
    block_table(len_ref, window_ref, flag_ref, pick_ref, tab_ref)
    for g in wd:
        g[1].end()
        g[2].start()

    def give(i, carry):
        def put(p, v):
            tok_out[i, :, p * BLK : (p + 1) * BLK] = v

        spread(tok_ref, pl.multiple_of((i * 2 + 1 - core) * SPAN, BLK), put)
        return carry

    def keep(i, carry):
        def put(p, v):
            tok[i, 0, :, p * BLK : (p + 1) * BLK] = v

        spread(tok_ref, pl.multiple_of((i * 2 + core) * SPAN, BLK), put)
        return carry

    lax.fori_loop(0, 4, give, 0)
    tok_swap = swap(tok_out, tok.at[:, 1], 0)
    tok_swap.start()
    lax.fori_loop(0, 4, keep, 0)

    kv[0:3] = jnp.zeros((3, BLK, WKV), BF16)
    kr[0:3] = jnp.zeros((3, BLK, 2 * BLK), BF16)


    for g in wd:
        g[2].middle()
    for g in ql:
        g[0].end()
        g[1].start()
    wkv_ring.start()
    wq_ring.start()
    tok_swap.wait_recv()
    for g in wd:
        g[2].end()

    def down(i, carry):
        t = tok[i].reshape(2 * BLK, 8 * BLK)
        first, second, third = (buf[i].reshape(NB, PIECE, BLK) for buf in wd_buf)
        shared = jnp.concatenate([first[:, 64:], second[:, 64:]], axis=1)
        packed = third[:, 64:].astype(F32)
        moved = pltpu.roll(packed.reshape(NB * 32, BLK), 64, 1).reshape(NB, 32, BLK)
        rope = jnp.concatenate([packed, moved], axis=1).astype(BF16)
        for lo, w in (
            (0, jnp.concatenate([first[:, :64], shared], axis=2)),
            (256, jnp.concatenate([second[:, :64], third[:, :64]], axis=2)),
            (512, rope),
        ):
            w = w.reshape(NB * 64, -1)
            part[:, :, lo : lo + w.shape[1]] += jnp.dot(
                t, w, preferred_element_type=F32
            ).reshape(2, BLK, -1)
        return carry

    part[...] = jnp.zeros_like(part)
    lax.fori_loop(0, 4, down, 0)
    part_swap = swap(part.at[1], part_in, 5)
    part_swap.start()
    wkv_ring.middle()
    part_swap.wait_recv()
    both = part[0] + part_in[...]
    latent = both[:, :KVL]
    norm = lax.rsqrt(jnp.mean(latent * latent, axis=1, keepdims=True) + 1e-06)
    place = tab_ref[c, 4]
    lane = lax.broadcasted_iota(jnp.int32, (BLK, BLK), 1)
    rope = both[:, KVL:]
    rope = jnp.where(lane < ROPE, rope, pltpu.roll(rope, 64, 1))
    own = jnp.concatenate(
        [latent * norm * gain_ref[...], turn(rope, cos_ref[place], sin_ref[place])], axis=1
    ).astype(BF16)
    kvn_a[y, x] = own[:HALF]
    kvn_b[y, x] = own[HALF:]
    for g in kvn:
        g[0].start()
    for g in kvn:
        g[0].end()
        g[1].start()
    for g in ql:
        g[1].middle()
    wkv_ring.end()
    wkv_swap = [swap(wkv.at[i, core], wkv.at[i, core], 1 + i) for i in range(4)]
    for s in wkv_swap:
        s.start()
    wq_ring.middle()
    wq_ring.end()
    wq_swap = [swap(wq.at[i, core], wq.at[i, core], 6 + i) for i in range(4)]
    for s in wq_swap:
        s.start()

    def arrival(me, j):
        return (me + j + j // 2 - 2 * (j // 3)) % 4

    wide = lax.broadcasted_iota(jnp.int32, (4 * HALF, BLK), 1)

    def line(along, j):
        if along == "y":
            return [(arrival(y, j), k) for k in range(4)]
        return [(k, arrival(x, j)) for k in range(4)]

    def queries(buf, row, along, first, last):
        rows = slice(row, row + HALF)

        def body(j, carry):
            places = line(along, j)
            left = jnp.concatenate([buf[p] for p in places], axis=0)
            places = [4 * yy + xx for yy, xx in places]
            flat = jnp.dot(left, wq[...].reshape(QL, WQ), preferred_element_type=F32)

            def put(slot, v):
                v = v.astype(BF16)
                for k, t in enumerate(places):
                    q[t, rows, slot * BLK : (slot + 1) * BLK] = v[k * HALF : (k + 1) * HALF]

            turns_of = [tab_ref[t, 4] for t in places]
            cosine = jnp.concatenate([cos_ref[p, rows] for p in turns_of], axis=0)
            sine = jnp.concatenate([sin_ref[p, rows] for p in turns_of], axis=0)
            for j in range(HL // 2):
                one, two, three = (flat[:, k * BLK : (k + 1) * BLK] for k in range(3 * j, 3 * j + 3))
                put(2 * j, one)
                put(2 * j + 1, jnp.where(wide < 64, pltpu.roll(two, 64, 1), pltpu.roll(three, 64, 1)))
                put(HL + j, turn(jnp.where(wide < 64, two, three), cosine, sine))
            return carry

        lax.fori_loop(first, last, body, 0)

    lane = lax.broadcasted_iota(jnp.int32, (HALF, BLK), 1)

    def keyvals(buf, row, along, first, last):
        rows = slice(row, row + HALF)

        def body(j, carry):
            places = line(along, j)
            left = [buf[p] for p in places]
            value = jnp.dot(
                jnp.concatenate([v[:, :KVL] for v in left], axis=0),
                wkv[...].reshape(KVL, WKV),
                preferred_element_type=F32,
            ).astype(BF16)
            for k, (yy, xx) in enumerate(places):
                t = 3 + 4 * yy + xx
                kv[t, rows, :] = value[k * HALF : (k + 1) * HALF]
                turned = left[k][:, KVL:].astype(F32)
                kr[t, rows, :BLK] = jnp.where(lane < ROPE, turned, 0.0).astype(BF16)
                kr[t, rows, BLK:] = jnp.where(lane < ROPE, 0.0, turned).astype(BF16)
            return carry

        lax.fori_loop(first, last, body, 0)

    for g in kvn:
        g[1].middle()
    for s in wkv_swap:
        s.wait_recv()
    keyvals(kvn_a, 0, "y", 0, 3)
    keyvals(kvn_b, HALF, "x", 0, 3)
    for s in wq_swap:
        s.wait_recv()
    queries(ql_a, 0, "y", 0, 3)
    queries(ql_b, HALF, "x", 0, 3)
    for g in kvn:
        g[1].end()
    keyvals(kvn_a, 0, "y", 3, 4)
    keyvals(kvn_b, HALF, "x", 3, 4)

    columns = pl.ds(pl.multiple_of(c * HL * BLK, HL * BLK), HL * BLK)

    def remote(i):
        return pltpu.make_async_remote_copy(
            src_ref=obuf.at[i],
            dst_ref=o_ref.at[:, columns],
            send_sem=asem.at[i],
            recv_sem=arem.at[i],
            device_id={"ctx": shifted(c, turns(i))},
            device_id_type=MESH,
        )

    def work(i):
        def write(h, value):
            obuf[i, :, h * BLK : (h + 1) * BLK] = value

        attend_block(shifted(c, turns(i)), tab_ref, q, kv, kr, write)

    def step(i, carry):
        @pl.when(i == 9)
        def _():
            for g in ql:
                g[1].end()
            queries(ql_a, 0, "y", 3, 4)
            queries(ql_b, HALF, "x", 3, 4)

        work(i)
        remote(i).start()
        return carry

    lax.fori_loop(1, NB, step, 0)
    work(0)
    local = pltpu.make_async_copy(obuf.at[0], o_ref.at[:, columns], asem.at[0])
    local.start()
    for g in wd + ql + kvn + [[wq_ring, wkv_ring]]:
        for s in g:
            s.sent()
    for s in [tok_swap, part_swap] + wkv_swap + wq_swap:
        s.wait_send()
    local.wait()

    def finish(i, carry):
        remote(i).wait()
        return carry

    lax.fori_loop(1, NB, finish, 0)


def tables():
    freq = np.exp(-math.log(10000.0) * 2.0 * np.arange(32, dtype=np.float32) / ROPE).astype(np.float32)
    phase = np.arange(MOST * BLK, dtype=np.float32)[:, None] * freq[None, :]
    cosine, sine = np.cos(phase.astype(np.float64)), np.sin(phase.astype(np.float64))
    shape = (MOST, BLK, BLK)
    return (
        np.concatenate([cosine] * 4, axis=1).astype(np.float32).reshape(shape),
        np.concatenate([-sine, sine, -sine, sine], axis=1).astype(np.float32).reshape(shape),
    )


def per_device(
    tokens,
    q_latent,
    w_down_kv,
    w_down_rope,
    kv_gain,
    w_up_q,
    w_up_kv,
    lengths,
    window,
    flags,
    anchor_pick,
):
    cosine, sine = tables()
    vmem = pl.BlockSpec(memory_space=pltpu.VMEM)
    n_sem = 4 * 19
    return pl.pallas_call(
        kernel,
        name="mla",
        out_shape=pltpu.VMEM((BLK, NB * HL * VDIM), BF16),
        in_specs=[pl.BlockSpec(memory_space=pltpu.SMEM)] * 4 + [vmem] * 9,
        out_specs=pl.BlockSpec(memory_space=pltpu.VMEM),
        scratch_shapes=[
            pltpu.VMEM((4, 4, 4, PIECE, BLK), BF16),
            pltpu.VMEM((4, 4, 4, PIECE, BLK), BF16),
            pltpu.VMEM((4, 4, 4, PIECE, BLK), BF16),
            pltpu.VMEM((4, 4, HALF, QL), BF16),
            pltpu.VMEM((4, 4, HALF, QL), BF16),
            pltpu.VMEM((4, 4, HALF, KVR), BF16),
            pltpu.VMEM((4, 4, HALF, KVR), BF16),
            pltpu.VMEM((4, 2, QL // 8, WQ), BF16),
            pltpu.VMEM((4, 2, KVL // 8, WKV), BF16),
            pltpu.VMEM((4, 2, BLK, 8 * BLK), BF16),
            pltpu.VMEM((4, BLK, 8 * BLK), BF16),
            pltpu.VMEM((2, BLK, KVR), F32),
            pltpu.VMEM((BLK, KVR), F32),
            pltpu.VMEM((NB, BLK, WQ), BF16),
            pltpu.VMEM((NB + 3, BLK, WKV), BF16),
            pltpu.VMEM((NB + 3, BLK, 2 * BLK), BF16),
            pltpu.VMEM((NB, BLK, HL * VDIM), BF16),
            pltpu.SMEM((NB, 8), jnp.int32),
            pltpu.SemaphoreType.DMA((n_sem,)),
            pltpu.SemaphoreType.DMA((n_sem,)),
            pltpu.SemaphoreType.DMA((10,)),
            pltpu.SemaphoreType.DMA((10,)),
            pltpu.SemaphoreType.DMA((NB,)),
            pltpu.SemaphoreType.DMA((NB,)),
        ],
        compiler_params=pltpu.CompilerParams(
            collective_id=1, has_side_effects=True, vmem_limit_bytes=56 * 2**20
        ),
    )(
        lengths,
        window,
        flags,
        anchor_pick,
        tokens,
        q_latent,
        w_down_kv,
        w_down_rope,
        w_up_q,
        w_up_kv,
        kv_gain.reshape(1, KVL),
        cosine,
        sine,
    )


def solution(mesh):
    return jax.shard_map(
        per_device,
        mesh=mesh,
        in_specs=(
            P(("batch", "ctx"), None),
            P(("batch", "ctx"), None),
            P(("batch", "ctx"), None),
            P(None, ("batch", "ctx")),
            P(),
            P("batch", "ctx"),
            P("batch", "ctx"),
            P("batch", None),
            P("batch", None),
            P("batch", None),
            P("batch", None),
        ),
        out_specs=P(("batch", "ctx"), None),
        check_vma=False,
    )
```

```python
import functools
import math

import jax
import jax.numpy as jnp
import numpy as np
from jax import lax
from jax.experimental import pallas as pl
from jax.experimental.pallas import tpu as pltpu
from jax.sharding import PartitionSpec as P

NOPE = 128
ROPE = 64
VDIM = 128
BLK = 128
HALF = BLK // 2
HL = 6
NB = 16
MOST = 8
KVL = 512
QL = 1536
D = 7168
SHARD = D // 128
SPAN = NB * SHARD
WQ = HL * (NOPE + ROPE)
WKV = HL * (NOPE + VDIM)
KVR = KVL + 2 * ROPE
MESH = pl.DeviceIdType.MESH
EXP_SCALE = (NOPE + ROPE) ** (-0.5) * math.log2(math.e)
LOW = -1e30
NT = (((1,), (1,)), ((), ()))
F32 = jnp.float32
BF16 = jnp.bfloat16
ORDERS = ("xyz", "yzx", "zxy")
PIECE = 96


def shifted(c, i):
    return ((c // 4 + i // 4) % 4) * 4 + (c % 4 + i % 4) % 4


def turns(n):
    j = n * 7 % 9
    near = 4 * (j // 3 + j // 6) + j % 3 + (j % 3) // 2
    j = (15 - n) % 7
    a = j // 2
    a, odd = a + a // 2 - 2 * (a // 3), j % 2
    far = 4 * (2 * (1 - odd) + a * odd) + a * (1 - odd) + 2 * odd
    late = n // 9
    return near * (1 - late) + far * late


class Ring:
    def __init__(self, block, half, me, plus, minus, ssem, rsem, base):
        def copy(ref, device, k):
            return pltpu.make_async_remote_copy(
                src_ref=ref,
                dst_ref=ref,
                send_sem=ssem.at[base + k],
                recv_sem=rsem.at[base + k],
                device_id=device,
                device_id_type=MESH,
            )

        self.up = copy(block(me), plus, 0)
        self.down = copy(block(me), minus, 1)
        self.on_up = copy(half((me + 3) % 4, 0), plus, 2)
        self.on_down = copy(half((me + 1) % 4, 1), minus, 3)

    def start(self):
        self.up.start()
        self.down.start()

    def middle(self):
        self.up.wait_recv()
        self.on_up.start()
        self.down.wait_recv()
        self.on_down.start()

    def end(self):
        self.on_up.wait_recv()
        self.on_down.wait_recv()

    def sent(self):
        for c in (self.up, self.down, self.on_up, self.on_down):
            c.wait_send()


class Direct:
    def __init__(self, block, me, others, ssem, rsem, base):
        ref = block(me)
        self.copies = [
            pltpu.make_async_remote_copy(
                src_ref=ref,
                dst_ref=ref,
                send_sem=ssem.at[base + k],
                recv_sem=rsem.at[base + k],
                device_id=other,
                device_id_type=MESH,
            )
            for k, other in enumerate(others)
        ]

    def start(self):
        for c in self.copies:
            c.start()

    def middle(self):
        pass

    def end(self):
        for c in self.copies:
            c.wait_recv()

    def sent(self):
        for c in self.copies:
            c.wait_send()


def block_table(len_ref, window_ref, flag_ref, pick_ref, tab_ref):
    starts, anchors, start = [], [], 0
    for s in range(4):
        length, rest = len_ref[0, s], pick_ref[0, s]
        for k in range(16, -1, -1):
            rest = jnp.where(rest >= length * 2**k, rest - length * 2**k, rest)
        anchors.append(jnp.where(flag_ref[0, s] == 1, start + rest, -1))
        starts.append(start)
        start = start + length
    for t in range(NB):
        row = [0, window_ref[0, 0], anchors[0]]
        for s in range(1, 4):
            later = starts[s] <= t
            row = [
                jnp.where(later, new, old)
                for new, old in zip((starts[s], window_ref[0, s], anchors[s]), row)
            ]
        for k in range(3):
            tab_ref[t, k] = row[k]
        tab_ref[t, 3] = jnp.clip(row[2], 0, NB - 1) + 3
        tab_ref[t, 4] = jnp.clip(t - row[0], 0, MOST - 1)


def turn(v, cosine, sine):
    lane = lax.broadcasted_iota(jnp.int32, v.shape, 1)
    other = jnp.where(lane % 64 < 32, pltpu.roll(v, 96, 1), pltpu.roll(v, 32, 1))
    return v * cosine + other * sine


def attend_block(t, tab_ref, q_ref, kv_ref, kr_ref, write):
    start, window, anchor = tab_ref[t, 0], tab_ref[t, 1], tab_ref[t, 2]
    bias = []
    for j in range(4):
        kb = t - 3 + j
        ok = (kb >= start) & ((window > 3 - j) | (kb == anchor))
        bias.append(jnp.where(ok, 0.0, LOW))
    bias.append(jnp.where((anchor >= 0) & (anchor < t - 3), 0.0, LOW))
    near_blocks, far = pl.ds(t, 4), tab_ref[t, 3]
    causal = lax.broadcasted_iota(jnp.int32, (BLK, BLK), 0) >= lax.broadcasted_iota(
        jnp.int32, (BLK, BLK), 1
    )

    def score(h):
        part, column = (h % 2) * BLK, 2 * h * BLK
        query = jnp.concatenate(
            [
                q_ref[t, :, h * BLK : (h + 1) * BLK],
                q_ref[t, :, (HL + h // 2) * BLK : (HL + h // 2 + 1) * BLK],
            ],
            axis=1,
        )
        near = jnp.concatenate(
            [
                kv_ref[near_blocks, :, column : column + BLK],
                kr_ref[near_blocks, :, part : part + BLK],
            ],
            axis=2,
        ).reshape(4 * BLK, 2 * BLK)
        last = jnp.concatenate(
            [kv_ref[far, :, column : column + BLK], kr_ref[far, :, part : part + BLK]], axis=1
        )
        keys = jnp.concatenate([near, last], axis=0)
        return lax.dot_general(query, keys, NT, preferred_element_type=F32)

    def weigh(scores):
        tiles = [scores[:, j * BLK : (j + 1) * BLK] + bias[j] for j in range(5)]
        tiles[3] = jnp.where(causal, tiles[3], LOW)
        top = functools.reduce(jnp.maximum, tiles)
        top = jnp.max(top, axis=1, keepdims=True)
        weights = [jnp.exp2((tile - top) * EXP_SCALE) for tile in tiles]
        total = jnp.sum(sum(weights[1:], weights[0]), axis=1, keepdims=True)
        return jnp.concatenate([w.astype(BF16) for w in weights], axis=1), total

    def mix(h, weights, total):
        column = (2 * h + 1) * BLK
        values = jnp.concatenate(
            [
                kv_ref[near_blocks, :, column : column + BLK].reshape(4 * BLK, BLK),
                kv_ref[far, :, column : column + BLK],
            ],
            axis=0,
        )
        return jnp.dot(weights, values, preferred_element_type=F32) / total

    scores = [score(h) for h in range(HL)]
    weighed = [weigh(s) for s in scores]
    for h in range(HL):
        write(h, mix(h, *weighed[h]).astype(BF16))


def spread(tok_ref, col, store):
    lane = lax.broadcasted_iota(jnp.int32, (BLK, BLK), 1)
    for p in range(8):
        tile, off = divmod(2 * SHARD * p, BLK)
        v = tok_ref[:, pl.ds(col + tile * BLK, BLK)].astype(F32)
        if off:
            v = pltpu.roll(v, BLK - off, 1)
            if tile < 6:
                after = tok_ref[:, pl.ds(col + (tile + 1) * BLK, BLK)].astype(F32)
                v = jnp.where(lane < BLK - off, v, pltpu.roll(after, BLK - off, 1))
        store(p, jnp.where(lane < 64, v, pltpu.roll(v, 8, 1)).astype(BF16))


def kernel(
    len_ref,
    window_ref,
    flag_ref,
    pick_ref,
    tok_ref,
    ql_ref,
    wd_ref,
    wr_ref,
    wq_ref,
    wkv_ref,
    gain_ref,
    cos_ref,
    sin_ref,
    o_ref,
    wd_a,
    wd_b,
    wd_c,
    ql_a,
    ql_b,
    kvn_a,
    kvn_b,
    wq,
    wkv,
    tok,
    tok_out,
    part,
    part_in,
    q,
    kv,
    kr,
    obuf,
    tab_ref,
    ssem,
    rsem,
    csem,
    cother,
    asem,
    arem,
):
    b, c = lax.axis_index("batch"), lax.axis_index("ctx")
    z, core, y, x = b // 2, b % 2, c // 4, c % 4
    at = {"x": x, "y": y, "z": z}

    def neighbour(axis, by):
        if axis == "x":
            return {"ctx": y * 4 + (x + by) % 4}
        if axis == "y":
            return {"ctx": ((y + by) % 4) * 4 + x}
        return {"batch": ((z + by) % 4) * 2 + core}

    partner = {"batch": z * 2 + 1 - core}

    barrier = pltpu.get_barrier_semaphore()
    peers = [{"ctx": shifted(c, i)} for i in range(1, NB)]
    peers += [neighbour("z", 1), neighbour("z", 2), neighbour("z", 3), partner]
    for peer in peers:
        pl.semaphore_signal(barrier, inc=1, device_id=peer, device_id_type=MESH)

    used = [0]

    def ring(axis, block, half):
        base = used[0]
        used[0] += 4
        return Ring(
            block, half, at[axis], neighbour(axis, 1), neighbour(axis, 3), ssem, rsem, base
        )

    def direct(axis, block):
        base = used[0]
        used[0] += 4
        return Direct(block, at[axis], [neighbour(axis, k) for k in (1, 2, 3)], ssem, rsem, base)

    def gather(buf, order, mid, dims="yx", quick=0):
        stages = []
        for i, axis in enumerate(order):
            done = order[:i]

            def block(k, axis=axis, done=done):
                index = [k if a == axis else slice(None) if a in done else at[a] for a in dims]
                return buf.at[tuple(index)]

            def half(k, h, axis=axis, done=done):
                index = [k if a == axis else slice(None) if a in done else at[a] for a in dims]
                return buf.at[tuple(index) + (pl.ds(h * mid, mid),)]

            stages.append(direct(axis, block) if i < quick else ring(axis, block, half))
        return stages

    def swap(src, dst, k):
        return pltpu.make_async_remote_copy(
            src_ref=src,
            dst_ref=dst,
            send_sem=csem.at[k],
            recv_sem=cother.at[k],
            device_id=partner,
            device_id_type=MESH,
        )

    wd_buf = (wd_a, wd_b, wd_c)
    wd = [gather(buf, order, PIECE // 2, "zyx", 2) for buf, order in zip(wd_buf, ORDERS)]
    ql = [gather(ql_a, "xy", 32), gather(ql_b, "yx", 32)]
    kvn = [gather(kvn_a, "xy", 32, quick=1), gather(kvn_b, "yx", 32, quick=1)]

    def up_ring(buf, rows):
        return ring(
            "z",
            lambda k: buf.at[k, core],
            lambda k, h: buf.at[k, core, pl.ds(h * rows // 2, rows // 2)],
        )

    wq_ring, wkv_ring = up_ring(wq, QL // 8), up_ring(wkv, KVL // 8)

    down_rows = jnp.concatenate([wd_ref[...].astype(F32), jnp.zeros((64 - SHARD, KVL), F32)], axis=0)
    rope_rows = lax.dot_general(
        (
            lax.broadcasted_iota(jnp.int32, (64, SHARD), 0)
            == lax.broadcasted_iota(jnp.int32, (64, SHARD), 1)
        ).astype(F32).astype(BF16),
        jnp.concatenate([wr_ref[...], wr_ref[...]], axis=0),
        NT,
        preferred_element_type=F32,
    )
    lane = lax.broadcasted_iota(jnp.int32, (32, BLK), 1)
    pieces = (
        (down_rows[:, :128], down_rows[:32, 128:256]),
        (down_rows[:, 256:384], down_rows[32:, 128:256]),
        (down_rows[:, 384:], jnp.where(lane < 64, rope_rows[:32], rope_rows[32:])),
    )
    for buf, piece in zip(wd_buf, pieces):
        buf[z, y, x] = jnp.concatenate(piece, axis=0).astype(BF16)

    pl.semaphore_wait(barrier, len(peers))
    for g in wd:
        g[0].start()
    ql_a[y, x] = ql_ref[:HALF]
    ql_b[y, x] = ql_ref[HALF:]
    for g in ql:
        g[0].start()
    for g in wd:
        g[0].end()
        g[1].start()
    wkv[z, core] = wkv_ref[...]
    wq[z, core] = wq_ref[...]
    for g in ql:
        g[0].middle()
    block_table(len_ref, window_ref, flag_ref, pick_ref, tab_ref)
    for g in wd:
        g[1].end()
        g[2].start()

    def give(i, carry):
        def put(p, v):
            tok_out[i, :, p * BLK : (p + 1) * BLK] = v

        spread(tok_ref, pl.multiple_of((i * 2 + 1 - core) * SPAN, BLK), put)
        return carry

    def keep(i, carry):
        def put(p, v):
            tok[i, 0, :, p * BLK : (p + 1) * BLK] = v

        spread(tok_ref, pl.multiple_of((i * 2 + core) * SPAN, BLK), put)
        return carry

    lax.fori_loop(0, 4, give, 0)
    tok_swap = swap(tok_out, tok.at[:, 1], 0)
    tok_swap.start()
    lax.fori_loop(0, 4, keep, 0)

    kv[0:3] = jnp.zeros((3, BLK, WKV), BF16)
    kr[0:3] = jnp.zeros((3, BLK, 2 * BLK), BF16)


    for g in wd:
        g[2].middle()
    for g in ql:
        g[0].end()
        g[1].start()
    wkv_ring.start()
    wq_ring.start()
    tok_swap.wait_recv()
    for g in wd:
        g[2].end()

    def down(i, carry):
        t = tok[i].reshape(2 * BLK, 8 * BLK)
        first, second, third = (buf[i].reshape(NB, PIECE, BLK) for buf in wd_buf)
        shared = jnp.concatenate([first[:, 64:], second[:, 64:]], axis=1)
        packed = third[:, 64:].astype(F32)
        moved = pltpu.roll(packed.reshape(NB * 32, BLK), 64, 1).reshape(NB, 32, BLK)
        rope = jnp.concatenate([packed, moved], axis=1).astype(BF16)
        for lo, w in (
            (0, jnp.concatenate([first[:, :64], shared], axis=2)),
            (256, jnp.concatenate([second[:, :64], third[:, :64]], axis=2)),
            (512, rope),
        ):
            w = w.reshape(NB * 64, -1)
            part[:, :, lo : lo + w.shape[1]] += jnp.dot(
                t, w, preferred_element_type=F32
            ).reshape(2, BLK, -1)
        return carry

    part[...] = jnp.zeros_like(part)
    lax.fori_loop(0, 4, down, 0)
    part_swap = swap(part.at[1], part_in, 5)
    part_swap.start()
    wkv_ring.middle()
    part_swap.wait_recv()
    both = part[0] + part_in[...]
    latent = both[:, :KVL]
    norm = lax.rsqrt(jnp.mean(latent * latent, axis=1, keepdims=True) + 1e-06)
    place = tab_ref[c, 4]
    lane = lax.broadcasted_iota(jnp.int32, (BLK, BLK), 1)
    rope = both[:, KVL:]
    rope = jnp.where(lane < ROPE, rope, pltpu.roll(rope, 64, 1))
    own = jnp.concatenate(
        [latent * norm * gain_ref[...], turn(rope, cos_ref[place], sin_ref[place])], axis=1
    ).astype(BF16)
    kvn_a[y, x] = own[:HALF]
    kvn_b[y, x] = own[HALF:]
    for g in kvn:
        g[0].start()
    for g in kvn:
        g[0].end()
        g[1].start()
    for g in ql:
        g[1].middle()
    wkv_ring.end()
    wkv_swap = [swap(wkv.at[i, core], wkv.at[i, core], 1 + i) for i in range(4)]
    for s in wkv_swap:
        s.start()
    wq_ring.middle()
    wq_ring.end()
    wq_swap = [swap(wq.at[i, core], wq.at[i, core], 6 + i) for i in range(4)]
    for s in wq_swap:
        s.start()

    def arrival(me, j):
        return (me + j + j // 2 - 2 * (j // 3)) % 4

    wide = lax.broadcasted_iota(jnp.int32, (4 * HALF, BLK), 1)

    def line(along, j):
        if along == "y":
            return [(arrival(y, j), k) for k in range(4)]
        return [(k, arrival(x, j)) for k in range(4)]

    def queries(buf, row, along, first, last):
        rows = slice(row, row + HALF)

        def body(j, carry):
            places = line(along, j)
            left = jnp.concatenate([buf[p] for p in places], axis=0)
            places = [4 * yy + xx for yy, xx in places]
            flat = jnp.dot(left, wq[...].reshape(QL, WQ), preferred_element_type=F32)

            def put(slot, v):
                v = v.astype(BF16)
                for k, t in enumerate(places):
                    q[t, rows, slot * BLK : (slot + 1) * BLK] = v[k * HALF : (k + 1) * HALF]

            turns_of = [tab_ref[t, 4] for t in places]
            cosine = jnp.concatenate([cos_ref[p, rows] for p in turns_of], axis=0)
            sine = jnp.concatenate([sin_ref[p, rows] for p in turns_of], axis=0)
            for j in range(HL // 2):
                one, two, three = (flat[:, k * BLK : (k + 1) * BLK] for k in range(3 * j, 3 * j + 3))
                put(2 * j, one)
                put(2 * j + 1, jnp.where(wide < 64, pltpu.roll(two, 64, 1), pltpu.roll(three, 64, 1)))
                put(HL + j, turn(jnp.where(wide < 64, two, three), cosine, sine))
            return carry

        lax.fori_loop(first, last, body, 0)

    lane = lax.broadcasted_iota(jnp.int32, (HALF, BLK), 1)

    def keyvals(buf, row, along, first, last):
        rows = slice(row, row + HALF)

        def body(j, carry):
            places = line(along, j)
            left = [buf[p] for p in places]
            value = jnp.dot(
                jnp.concatenate([v[:, :KVL] for v in left], axis=0),
                wkv[...].reshape(KVL, WKV),
                preferred_element_type=F32,
            ).astype(BF16)
            for k, (yy, xx) in enumerate(places):
                t = 3 + 4 * yy + xx
                kv[t, rows, :] = value[k * HALF : (k + 1) * HALF]
                turned = left[k][:, KVL:].astype(F32)
                kr[t, rows, :BLK] = jnp.where(lane < ROPE, turned, 0.0).astype(BF16)
                kr[t, rows, BLK:] = jnp.where(lane < ROPE, 0.0, turned).astype(BF16)
            return carry

        lax.fori_loop(first, last, body, 0)

    for g in kvn:
        g[1].middle()
    for s in wkv_swap:
        s.wait_recv()
    keyvals(kvn_a, 0, "y", 0, 3)
    keyvals(kvn_b, HALF, "x", 0, 3)
    for s in wq_swap:
        s.wait_recv()
    queries(ql_a, 0, "y", 0, 3)
    queries(ql_b, HALF, "x", 0, 3)
    for g in kvn:
        g[1].end()
    keyvals(kvn_a, 0, "y", 3, 4)
    keyvals(kvn_b, HALF, "x", 3, 4)

    columns = pl.ds(pl.multiple_of(c * HL * BLK, HL * BLK), HL * BLK)

    def remote(i):
        return pltpu.make_async_remote_copy(
            src_ref=obuf.at[i],
            dst_ref=o_ref.at[:, columns],
            send_sem=asem.at[i],
            recv_sem=arem.at[i],
            device_id={"ctx": shifted(c, turns(i))},
            device_id_type=MESH,
        )

    def work(i):
        def write(h, value):
            obuf[i, :, h * BLK : (h + 1) * BLK] = value

        attend_block(shifted(c, turns(i)), tab_ref, q, kv, kr, write)

    def step(i, carry):
        @pl.when(i == 9)
        def _():
            for g in ql:
                g[1].end()
            queries(ql_a, 0, "y", 3, 4)
            queries(ql_b, HALF, "x", 3, 4)

        work(i)
        remote(i).start()
        return carry

    lax.fori_loop(1, NB, step, 0)
    work(0)
    local = pltpu.make_async_copy(obuf.at[0], o_ref.at[:, columns], asem.at[0])
    local.start()
    for g in wd + ql + kvn + [[wq_ring, wkv_ring]]:
        for s in g:
            s.sent()
    for s in [tok_swap, part_swap] + wkv_swap + wq_swap:
        s.wait_send()
    local.wait()

    def finish(i, carry):
        remote(i).wait()
        return carry

    lax.fori_loop(1, NB, finish, 0)


def tables():
    freq = np.exp(-math.log(10000.0) * 2.0 * np.arange(32, dtype=np.float32) / ROPE).astype(np.float32)
    phase = np.arange(MOST * BLK, dtype=np.float32)[:, None] * freq[None, :]
    cosine, sine = np.cos(phase.astype(np.float64)), np.sin(phase.astype(np.float64))
    shape = (MOST, BLK, BLK)
    return (
        np.concatenate([cosine] * 4, axis=1).astype(np.float32).reshape(shape),
        np.concatenate([-sine, sine, -sine, sine], axis=1).astype(np.float32).reshape(shape),
    )


def per_device(
    tokens,
    q_latent,
    w_down_kv,
    w_down_rope,
    kv_gain,
    w_up_q,
    w_up_kv,
    lengths,
    window,
    flags,
    anchor_pick,
):
    cosine, sine = tables()
    vmem = pl.BlockSpec(memory_space=pltpu.VMEM)
    n_sem = 4 * 19
    return pl.pallas_call(
        kernel,
        name="mla",
        out_shape=pltpu.VMEM((BLK, NB * HL * VDIM), BF16),
        in_specs=[pl.BlockSpec(memory_space=pltpu.SMEM)] * 4 + [vmem] * 9,
        out_specs=pl.BlockSpec(memory_space=pltpu.VMEM),
        scratch_shapes=[
            pltpu.VMEM((4, 4, 4, PIECE, BLK), BF16),
            pltpu.VMEM((4, 4, 4, PIECE, BLK), BF16),
            pltpu.VMEM((4, 4, 4, PIECE, BLK), BF16),
            pltpu.VMEM((4, 4, HALF, QL), BF16),
            pltpu.VMEM((4, 4, HALF, QL), BF16),
            pltpu.VMEM((4, 4, HALF, KVR), BF16),
            pltpu.VMEM((4, 4, HALF, KVR), BF16),
            pltpu.VMEM((4, 2, QL // 8, WQ), BF16),
            pltpu.VMEM((4, 2, KVL // 8, WKV), BF16),
            pltpu.VMEM((4, 2, BLK, 8 * BLK), BF16),
            pltpu.VMEM((4, BLK, 8 * BLK), BF16),
            pltpu.VMEM((2, BLK, KVR), F32),
            pltpu.VMEM((BLK, KVR), F32),
            pltpu.VMEM((NB, BLK, WQ), BF16),
            pltpu.VMEM((NB + 3, BLK, WKV), BF16),
            pltpu.VMEM((NB + 3, BLK, 2 * BLK), BF16),
            pltpu.VMEM((NB, BLK, HL * VDIM), BF16),
            pltpu.SMEM((NB, 8), jnp.int32),
            pltpu.SemaphoreType.DMA((n_sem,)),
            pltpu.SemaphoreType.DMA((n_sem,)),
            pltpu.SemaphoreType.DMA((10,)),
            pltpu.SemaphoreType.DMA((10,)),
            pltpu.SemaphoreType.DMA((NB,)),
            pltpu.SemaphoreType.DMA((NB,)),
        ],
        compiler_params=pltpu.CompilerParams(
            collective_id=1, has_side_effects=True, vmem_limit_bytes=56 * 2**20
        ),
    )(
        lengths,
        window,
        flags,
        anchor_pick,
        tokens,
        q_latent,
        w_down_kv,
        w_down_rope,
        w_up_q,
        w_up_kv,
        kv_gain.reshape(1, KVL),
        cosine,
        sine,
    )


def solution(mesh):
    return jax.shard_map(
        per_device,
        mesh=mesh,
        in_specs=(
            P(("batch", "ctx"), None),
            P(("batch", "ctx"), None),
            P(("batch", "ctx"), None),
            P(None, ("batch", "ctx")),
            P(),
            P("batch", "ctx"),
            P("batch", "ctx"),
            P("batch", None),
            P("batch", None),
            P("batch", None),
            P("batch", None),
        ),
        out_specs=P(("batch", "ctx"), None),
        check_vma=False,
    )
```
